32 devices in a mesh: groups: 2 (over y), sx: 4 (over z), sy: 2 (over x), sz: 2 (over core).
Axes of the slice: x: 2, y: 2, z: 4, core: 2. Of those that a mesh axis runs over, the one named last changes fastest.
Arguments:
- prior: float32 [128, 32, 16, 256], P(None, ('groups', 'sx'), ('sy', 'sz')), parts along dimension 1, may hold values from -6 to 6
- current: float32 [64, 32, 16, 256], P(None, ('groups', 'sx'), ('sy', 'sz')), parts along dimension 1, may hold values from -150 to 150
- site_xy: float32 [2, 32, 16, 256], P(None, ('groups', 'sx'), ('sy', 'sz')), parts along dimension 1, may hold values from 0 to 1
- links: int32 [9, 32, 16], P(None, ('groups', 'sx'), ('sy', 'sz')), parts along dimension 1, may hold values from 0 to 1, as said below
Outputs:
- first_block: float32 [64, 32, 16, 256], P(None, ('groups', 'sx'), ('sy', 'sz')), parts along dimension 1
- second_block: float32 [64, 32, 16, 256], P(None, ('groups', 'sx'), ('sy', 'sz')), parts along dimension 1
The draws below stay inside these ranges and needn't reach their ends.
There are 2 independent parts, one for each index of `groups`. The reference program is written for one: setup_inputs(seed, part) draws one part's arguments, and reference() takes and returns one part's arrays. A program takes and returns all parts, laid end to end along the dimension named above; each array names one. Nothing has to cross between parts.
Inputs may be any that keep to these rules, and one draw needn't show every extreme that they name: links[o] of a tile equals links[8 - o] of the tile it points to; links[4] is 1; links that point out of the grid are 0.
All inputs are finite; a program needn't handle non-finite values.
Results may differ from the reference program's by a relative error of at most 0.00027.
Values sent between devices are 32-bit elements; how exact they have to be, the bound alone decides.
A program may use at most 64 MiB of HBM per device.

```python
import jax
import jax.numpy as jnp
from jax import lax

TS = 256
BLOCK = 64
PREV = 128
TX = 16
TY = 16
SITES = 65536


def draw_current(key, part):
    key = jax.random.fold_in(key, 7)
    values = jnp.clip(jax.random.normal(key, (BLOCK, TX, TY, TS), jnp.float32), -5.0, 5.0)
    rising = 1.0 + 2.0 * jnp.arange(TX, dtype=jnp.float32) / max(TX - 1, 1)
    values = values * rising[None, :, None, None]
    return values


def draw_links(key, part):
    key = jax.random.fold_in(key, 11)
    picks = jax.random.randint(key, (4, TX, TY), 0, 10)
    chosen = jnp.where(picks < 7, 1, 0).astype(jnp.int32)
    rows = jnp.arange(TX, dtype=jnp.int32)[:, None]
    cols = jnp.arange(TY, dtype=jnp.int32)[None, :]
    result = [None] * 9
    result[4] = jnp.ones((TX, TY), jnp.int32)
    for index, code in enumerate([5, 6, 7, 8]):
        shift_x = code // 3 - 1
        shift_y = code % 3 - 1
        inside = (rows + shift_x >= 0) & (rows + shift_x < TX) & (cols + shift_y >= 0) & (cols + shift_y < TY)
        forward = chosen[index] * inside.astype(jnp.int32)
        result[code] = forward
        padded = jnp.pad(forward, 1)
        result[8 - code] = padded[1 - shift_x:1 - shift_x + TX, 1 - shift_y:1 - shift_y + TY]
    return jnp.stack(result, axis=0)


def level_of(key, shape, split, least, top_value):
    level, own = 1.0, jax.random.fold_in(key, 6)
    for position, parts in split:
        steps = jnp.exp(jax.random.uniform(jax.random.fold_in(own, position), (parts,), jnp.float32, least / len(split), top_value / len(split)))
        level = level * jnp.repeat(steps, shape[position] // parts).reshape([-1 if axis == position else 1 for axis in range(len(shape))])
    return level


def scatter_about(rng, extent, deviation, most, cuts=(), kind=jnp.bfloat16):
    drawn = jax.random.normal(rng, extent, jnp.float32) * deviation
    if len(cuts) > 0:
        drawn = level_of(rng, extent, cuts, -0.22, 0.18) * drawn
    return jnp.clip(drawn, min=-most, max=most).astype(kind)


def setup_inputs(seed: int = 0, part: int = 0) -> dict:
    keys = jax.random.split(jax.random.key(seed), 5)
    part_splits = jax.random.split(jax.random.fold_in(keys[4], part), 5)
    prior = scatter_about(part_splits[0], (PREV, TX, TY, TS), 1.0, 6.0, ((1, 4), (2, 4)), jnp.float32)
    current = draw_current(jax.random.fold_in(jax.random.fold_in(keys[4], part), 71), part)
    site_xy = jnp.clip(1.0 * jax.random.uniform(part_splits[2], (2, TX, TY, TS), jnp.float32) ** level_of(part_splits[2], (2, TX, TY, TS), ((1, 4), (2, 4)), -0.2, 0.2), 0.0, 1.0)
    links = draw_links(jax.random.fold_in(jax.random.fold_in(keys[4], part), 71), part)
    return dict(prior=prior, current=current, site_xy=site_xy, links=links)


kernel_gain = 0.0625

def lower_solve(lower, rhs):
    return lax.linalg.triangular_solve(lower, rhs, left_side=True, lower=True)

def kernel_weights(own, near, shift_x, shift_y, link):
    delta_x = own[0][..., :, None] - near[0][..., None, :] - shift_x
    delta_y = own[1][..., :, None] - near[1][..., None, :] - shift_y
    dist = jnp.sqrt(delta_x * delta_x + delta_y * delta_y)
    fall = jnp.maximum(1.0 - dist, 0.0)
    return fall ** 4 * (4.0 * dist + 1.0) * kernel_gain * link[..., None, None]

def apply_kernel(vectors, places, links):
    count = vectors.shape[0]
    tiles_x = vectors.shape[1]
    tiles_y = vectors.shape[2]
    joined = jnp.concatenate([vectors, places], axis=0)
    padded = jnp.pad(joined, ((0, 0), (1, 1), (1, 1), (0, 0)))
    link_f = links.astype(places.dtype)

    def one_row(row):
        own = lax.dynamic_slice_in_dim(places, row, 1, 1)[:, 0]
        band = lax.dynamic_slice_in_dim(padded, row, 3, 1)
        row_links = lax.dynamic_slice_in_dim(link_f, row, 1, 1)[:, 0]
        total = jnp.zeros((count, tiles_y, vectors.shape[3]), vectors.dtype)
        for code in range(9):
            shift_x = code // 3 - 1
            shift_y = code % 3 - 1
            near = band[:, shift_x + 1, 1 + shift_y:1 + shift_y + tiles_y]
            weights = kernel_weights(own, near[count:], shift_x, shift_y, row_links[code])
            total = total + jnp.einsum('yij,myj->myi', weights, near[:count], precision=lax.Precision.HIGHEST)
        return total
    rows = lax.map(one_row, jnp.arange(tiles_x, dtype=jnp.int32))
    return jnp.transpose(rows, (1, 0, 2, 3))

def lanczos_step(basis, block, places, links):
    image = apply_kernel(block, places, links)
    span = jnp.concatenate([basis, block], axis=0)
    flat_span = span.reshape(span.shape[0], -1)
    flat_image = image.reshape(block.shape[0], -1)
    coef = jnp.dot(flat_span.astype(jnp.float32), flat_image.T.astype(jnp.float32), precision=lax.Precision.HIGHEST, preferred_element_type=jnp.float32) / SITES
    flat_image = flat_image - jnp.dot(coef.T.astype(jnp.float32), flat_span.astype(jnp.float32), precision=lax.Precision.HIGHEST, preferred_element_type=jnp.float32)
    gram = jnp.dot(flat_image.astype(jnp.float32), flat_image.T.astype(jnp.float32), precision=lax.Precision.HIGHEST, preferred_element_type=jnp.float32) / SITES
    lower = jnp.linalg.cholesky(gram)
    fresh = lower_solve(lower, flat_image)
    return fresh.reshape(block.shape)

def reference(prior, current, site_xy, links):
    first_block = lanczos_step(prior, current, site_xy, links)
    widened = jnp.concatenate([prior, current], axis=0)
    second_block = lanczos_step(widened, first_block, site_xy, links)
    return (first_block, second_block)
```

```python
import functools

import jax
import jax.numpy as jnp
from jax import lax
from jax.experimental import pallas as pl
from jax.experimental.pallas import tpu as pltpu
from jax.sharding import PartitionSpec as P

GAIN = 0.0625
MESH = pl.DeviceIdType.MESH
F32 = jnp.float32
BF16 = jnp.bfloat16
HIGH = lax.Precision.HIGHEST
DIRS = [(da, db) for da in (-1, 0, 1) for db in (-1, 0, 1) if (da, db) != (0, 0)]


def dot_nn(left, right):
    return lax.dot_general(
        left, right, (((1,), (0,)), ((), ())), precision=HIGH, preferred_element_type=F32
    )


def dot_nt(left, right):
    return lax.dot_general(
        left, right, (((1,), (1,)), ((), ())), precision=HIGH, preferred_element_type=F32
    )


def dot_fast(left, right):
    return lax.dot_general(
        left, right, (((1,), (0,)), ((), ())), preferred_element_type=F32
    )


def inverse_factor(gram):
    size = gram.shape[0]
    rows = lax.broadcasted_iota(jnp.int32, (size, size), 0)
    cols = lax.broadcasted_iota(jnp.int32, (size, size), 1)
    eye = jnp.where(rows == cols, 1.0, 0.0).astype(F32)
    work = jnp.concatenate([eye, gram], axis=1)
    wide = 2 * size
    rowid = lax.broadcasted_iota(jnp.int32, (size, wide), 0)
    pivots = jnp.ones((size, wide), F32)
    panel = 8
    for base in range(0, size, panel):
        cast = [
            jnp.broadcast_to(work[:, size + base + c : size + base + c + 1], (size, wide))
            for c in range(panel)
        ]
        for c in range(panel):
            k = base + c
            pivot = cast[c][k : k + 1, :]
            pivots = jnp.where(rowid == k, pivot, pivots)
            factor = jnp.where(rowid > k, cast[c] * (1.0 / pivot), 0.0)
            work = work - factor * work[k : k + 1, :]
            for d in range(c + 1, panel):
                cast[d] = cast[d] - factor * cast[d][k : k + 1, :]
    scaled = work * lax.rsqrt(pivots)
    return scaled[:, :size]


def body(
    nsx, nsy, nsz, tx, ty,
    links, prior_in, cur_in, pos_in,
    first_out, second_out,
    khi, klo, span, vpad, vbf, ppad, ncol, grams, mix,
    ss_x, ss_a, ss_b, ss_z, ss_y,
    r1_x, r1_a, r1_b, r1_z, r1_y,
    r2_x, r2_a, r2_b, r2_z, r2_y,
    load_sem, pos_s, pos_r, v1_s, v1_r, v2_s, v2_r, pl_s, pl_r, z_s, z_r, g_s, g_r,
):
    nq = nsy * nsz
    group = lax.axis_index("groups")
    sx = lax.axis_index("sx")
    q = lax.axis_index("sy") * nsz + lax.axis_index("sz")
    prev = prior_in.shape[1]
    width = cur_in.shape[1]
    total_sites = float(tx * ty * 256 * nsx * nq)
    tiles = tx * ty

    def device(s, p):
        return (group, s, p // nsz, lax.rem(p, nsz))

    def exists(d):
        s, p = sx + d[0], q + d[1]
        return (s >= 0) & (s < nsx) & (p >= 0) & (p < nq)

    loads = []
    for a in range(tx):
        loads.append(pltpu.make_async_copy(
            cur_in.at[pl.ds(a * ty, ty)], vpad.at[a + 1, pl.ds(1, ty)], load_sem.at[a]))
        loads.append(pltpu.make_async_copy(
            pos_in.at[pl.ds(a * ty, ty)], ppad.at[a + 1, pl.ds(1, ty)], load_sem.at[tx + a]))
    prior_load = pltpu.make_async_copy(prior_in, span.at[:, pl.ds(0, prev)], load_sem.at[2 * tx])
    cur_load = pltpu.make_async_copy(
        cur_in, span.at[:, pl.ds(prev + width, width)], load_sem.at[2 * tx + 1])
    for a in range(tx + 2):
        for b in range(ty + 2):
            if a in (0, tx + 1) or b in (0, ty + 1):
                vpad[a, b] = jnp.zeros((width, 256), F32)
                ppad[a, b] = jnp.zeros((2, 256), F32)
    for load in loads:
        load.start()
    prior_load.start()
    cur_load.start()

    barrier = pltpu.get_barrier_semaphore()
    expected = jnp.int32(nq - 1 + nsx - 1)
    for d in DIRS:
        ok = exists(d)
        expected = expected + jnp.where(ok, 1, 0)

        @pl.when(ok)
        def _(d=d):
            pl.semaphore_signal(
                barrier, inc=1, device_id=device(sx + d[0], q + d[1]), device_id_type=MESH)
    for k in range(1, nq):
        pl.semaphore_signal(
            barrier, inc=1, device_id=device(sx, lax.rem(q + k, nq)), device_id_type=MESH)
    for k in range(1, nsx):
        pl.semaphore_signal(
            barrier, inc=1, device_id=device(lax.rem(sx + k, nsx), q), device_id_type=MESH)
    pl.semaphore_wait(barrier, expected)
    for load in loads:
        load.wait()

    def pick(shift, count):
        src = {-1: pl.ds(1, 1), 0: pl.ds(1, count), 1: pl.ds(count, 1)}[shift]
        dst = {-1: pl.ds(count + 1, 1), 0: pl.ds(1, count), 1: pl.ds(0, 1)}[shift]
        return src, dst

    def halo_copy(ref, i, send, recv):
        d = DIRS[i]
        (sa, da), (sb, db) = pick(d[0], tx), pick(d[1], ty)
        return pltpu.make_async_remote_copy(
            src_ref=ref.at[sa, sb], dst_ref=ref.at[da, db],
            send_sem=send.at[i], recv_sem=recv.at[i],
            device_id=device(sx + d[0], q + d[1]), device_id_type=MESH)

    def halo_start(ref, send, recv):
        for i, d in enumerate(DIRS):
            @pl.when(exists(d))
            def _(i=i):
                halo_copy(ref, i, send, recv).start()

    def halo_wait(ref, send, recv):
        for i, d in enumerate(DIRS):
            @pl.when(exists(d))
            def _(i=i):
                halo_copy(ref, i, send, recv).wait_send()

            @pl.when(exists((-d[0], -d[1])))
            def _(i=i):
                halo_copy(ref, i, send, recv).wait_recv()

    class Reduce:
        def __init__(self, which, x, a, b, z, y):
            self.w, self.x, self.a, self.b, self.z, self.y = which, x, a, b, z, y

        def plane(self, k):
            to = lax.rem(q + k, nq)
            return pltpu.make_async_remote_copy(
                src_ref=self.x.at[to], dst_ref=self.a.at[k - 1],
                send_sem=pl_s.at[self.w, k - 1], recv_sem=pl_r.at[self.w, k - 1],
                device_id=device(sx, to), device_id_type=MESH)

        def line(self, k):
            to = lax.rem(sx + k, nsx)
            return pltpu.make_async_remote_copy(
                src_ref=self.z, dst_ref=self.b.at[sx],
                send_sem=z_s.at[self.w, k - 1], recv_sem=z_r.at[self.w, k - 1],
                device_id=device(to, q), device_id_type=MESH)

        def back(self, k):
            to = lax.rem(q + k, nq)
            return pltpu.make_async_remote_copy(
                src_ref=self.y.at[q], dst_ref=self.y.at[q],
                send_sem=g_s.at[self.w, k - 1], recv_sem=g_r.at[self.w, k - 1],
                device_id=device(sx, to), device_id_type=MESH)

        def start(self):
            for k in range(1, nq):
                self.plane(k).start()

        def second(self):
            for k in range(1, nq):
                self.plane(k).wait()
            part = self.x[q]
            for k in range(1, nq):
                part = part + self.a[k - 1]
            self.z[...] = part
            for k in range(1, nsx):
                self.line(k).start()
            self.b[sx] = part

        def third(self):
            for k in range(1, nsx):
                self.line(k).wait()
            part = self.b[0]
            for k in range(1, nsx):
                part = part + self.b[k]
            self.y[q] = part * (1.0 / total_sites)
            for k in range(1, nq):
                self.back(k).start()

        def finish(self):
            for k in range(1, nq):
                self.back(k).wait()

    reduce_ss = Reduce(0, ss_x, ss_a, ss_b, ss_z, ss_y)
    reduce_1 = Reduce(1, r1_x, r1_a, r1_b, r1_z, r1_y)
    reduce_2 = Reduce(2, r2_x, r2_a, r2_b, r2_z, r2_y)

    halo_start(ppad, pos_s, pos_r)
    halo_start(vpad, v1_s, v1_r)

    def split(a, b):
        value = vpad[a, b]
        high = value.astype(BF16)
        vbf[a, b, 0:width] = high
        vbf[a, b, width : 2 * width] = (value - high.astype(F32)).astype(BF16)

    def interior(a, b):
        return (a >= 1) & (a <= tx) & (b >= 1) & (b <= ty)

    def make_block(na, nb, code):
        da, db = code // 3 - 1, code % 3 - 1
        oa, ob = na - da, nb - db
        own = (oa - 1) * ty + (ob - 1)

        @pl.when(interior(oa, ob))
        def _():
            link = links[code * tiles + own].astype(F32) * GAIN
            c1 = link
            c4 = link * 4.0
            place = own * 9 + code
            xrow = ppad[oa, ob, 0:1, :] - float(da)
            yrow = ppad[oa, ob, 1:2, :] - float(db)
            step = 32
            for j in range(0, 256, step):
                nx = ncol[0, j : j + step, :]
                ny = ncol[1, j : j + step, :]
                for half in range(0, 256, 128):
                    dx = nx - xrow[:, half : half + 128]
                    dy = ny - yrow[:, half : half + 128]
                    sq = dx * dx + dy * dy
                    dist = sq * lax.rsqrt(jnp.maximum(sq, 1e-30))
                    fall = jnp.maximum(1.0 - dist, 0.0)
                    two = fall * fall
                    value = (two * two) * (dist * c4 + c1)
                    high = value.astype(BF16)
                    khi[place, j : j + step, half : half + 128] = high
                    klo[place, j : j + step, half : half + 128] = (
                        value - high.astype(F32)).astype(BF16)
            apply_block(na, nb, place, own, prev)

    def apply_block(na, nb, place, own, base):
        both = dot_fast(vbf[na, nb], khi[place])
        low = dot_fast(vbf[na, nb, 0:width], klo[place])
        rows = pl.ds(base, width)
        span[own, rows] = span[own, rows] + (both[0:width] + both[width : 2 * width] + low)

    def make_near(na, nb):
        split(na, nb)
        for c in range(2):
            row = ppad[na, nb, c : c + 1, :]
            ncol[c] = jnp.transpose(jnp.broadcast_to(row, (128, 256)))
        for code in range(9):
            make_block(na, nb, code)

    def clear(t, base):
        span[t, pl.ds(base, width)] = jnp.zeros((width, 256), F32)

    @pl.loop(0, tiles)
    def _(t):
        clear(t, prev)
        clear(t, prev + 2 * width)

    prior_load.wait()
    cur_load.wait()
    full = prev + 2 * width
    for part in range(2):
        grams[...] = jnp.zeros_like(grams)
        rows = pl.ds(0, prev) if part == 0 else pl.ds(prev + width, width)
        size = prev if part == 0 else width

        @pl.loop(0, tiles)
        def _(t):
            grams[0:size, :] = grams[0:size, :] + dot_nt(span[t, rows], span[t, 0:full])
        chunk = ss_x.shape[1]
        offset = 0 if part == 0 else prev
        for r in range(0, size, 8):
            c, i = (offset + r) // chunk, (offset + r) % chunk
            ss_x[c, i : i + 8] = grams[r : r + 8, :]
    reduce_ss.start()

    @pl.loop(1, tx + 1)
    def _(a):
        @pl.loop(1, ty + 1)
        def _(b):
            make_near(a, b)

        @pl.when(a == 1)
        def _():
            reduce_ss.second()

        @pl.when(a == 2)
        def _():
            reduce_ss.third()

        @pl.when(a == 3)
        def _():
            reduce_ss.finish()

    halo_wait(ppad, pos_s, pos_r)
    halo_wait(vpad, v1_s, v1_r)

    @pl.loop(0, tx + 2)
    def _(a):
        @pl.loop(0, ty + 2)
        def _(b):
            @pl.when(jnp.logical_not(interior(a, b)))
            def _():
                make_near(a, b)

    def products(base, x, extra):
        grams[0:width, :] = jnp.zeros((width, full), F32)
        if extra:
            grams[width : 2 * width, :] = jnp.zeros((width, full), F32)

        @pl.loop(0, tiles)
        def _(t):
            image = span[t, pl.ds(base, width)]
            grams[0:width, :] = grams[0:width, :] + dot_nt(image, span[t, 0:full])
            if extra:
                grams[width : 2 * width, 0:width] = (
                    grams[width : 2 * width, 0:width] + dot_nt(image, image))
        chunk = x.shape[1]
        for c in range(nq):
            x[c, :, 0:full] = grams[c * chunk : (c + 1) * chunk, :]
            if extra:
                x[c, :, full : full + 128] = grams[
                    width + c * chunk : width + (c + 1) * chunk, 0:128]

    products(prev, r1_x, False)
    reduce_1.start()
    reduce_1.second()
    reduce_1.third()
    reduce_1.finish()

    chunk = ss_x.shape[1]
    grams[prev : prev + width, :] = jnp.zeros((width, full), F32)
    for r in range(0, prev + width, 8):
        c, i = r // chunk, r % chunk
        row = r if r < prev else r + width
        grams[row : row + 8, :] = ss_y[c, i : i + 8]
    lane = lax.broadcasted_iota(jnp.int32, (width, full), 1)
    inside = (lane >= prev) & (lane < prev + width)
    tlane = lax.broadcasted_iota(jnp.int32, (full, full), 1)
    grams[...] = jnp.where((tlane >= prev) & (tlane < prev + width), 0.0, grams[...])

    red = jnp.concatenate([r1_y[c] for c in range(nq)], axis=0)
    coef = jnp.where(inside, 0.0, red)
    over = dot_nn(coef, grams[...])
    gram = red[:, prev : prev + width] + dot_nt(over - 2.0 * coef, coef)
    lower = inverse_factor(gram)
    mix[:, 0:full] = -dot_nn(lower, coef)
    mix[:, prev : prev + width] = lower
    cross = dot_nn(lower, coef - over)

    @pl.loop(0, tiles)
    def _(t):
        fresh = dot_nn(mix[:, 0:full], span[t, 0:full])
        first_out[t] = fresh
        span[t, pl.ds(prev, width)] = fresh
        vpad[t // ty + 1, lax.rem(t, ty) + 1] = fresh

    halo_start(vpad, v2_s, v2_r)
    rowi = lax.broadcasted_iota(jnp.int32, (width, full), 0)
    cross = jnp.where(lane == rowi + prev, 1.0, cross)
    cross_t = jnp.transpose(cross)
    grams[prev : prev + width, :] = cross
    grams[:, prev : prev + width] = cross_t
    tmat = grams[...]

    def second_apply(inner):
        @pl.loop(0, tiles)
        def _(t):
            oa, ob = t // ty + 1, lax.rem(t, ty) + 1
            for code in range(9):
                na, nb = oa + code // 3 - 1, ob + code % 3 - 1
                use = interior(na, nb) if inner else jnp.logical_not(interior(na, nb))

                @pl.when(use)
                def _(na=na, nb=nb, code=code):
                    apply_block(na, nb, t * 9 + code, t, prev + 2 * width)

    def split_all(inner):
        @pl.loop(0, tx + 2)
        def _(a):
            @pl.loop(0, ty + 2)
            def _(b):
                use = interior(a, b) if inner else jnp.logical_not(interior(a, b))

                @pl.when(use)
                def _():
                    split(a, b)

    mix[:, full : full + 128] = jnp.zeros((width, 128), F32)
    ss_keep = tmat
    split_all(True)
    second_apply(True)
    halo_wait(vpad, v2_s, v2_r)
    split_all(False)
    second_apply(False)

    products(prev + 2 * width, r2_x, True)
    grams[...] = ss_keep
    reduce_2.start()
    reduce_2.second()
    reduce_2.third()
    reduce_2.finish()
    red = jnp.concatenate([r2_y[c] for c in range(nq)], axis=0)
    coef = red[:, 0:full]
    over = dot_nn(coef, grams[...])
    gram = red[:, full : full + width] + dot_nt(over - 2.0 * coef, coef)
    lower = inverse_factor(gram)
    mix[:, 0:full] = -dot_nn(lower, coef)
    mix[:, full : full + width] = lower

    @pl.loop(0, tiles)
    def _(t):
        second_out[t] = dot_nn(mix[:, 0:full], span[t, 0:full]) + dot_nn(
            mix[:, full : full + width], span[t, full : full + width])


def on_device(nsx, nsy, nsz, prior, current, site_xy, links):
    prev, tx, ty, ts = prior.shape
    width = current.shape[0]
    tiles = tx * ty
    nq = nsy * nsz
    full = prev + 2 * width

    def tiled(x):
        return jnp.transpose(x.reshape(x.shape[0], tiles, ts), (1, 0, 2))

    def reduce_bufs(rows, cols):
        chunk = rows // nq
        return [
            pltpu.VMEM((nq, chunk, cols), F32),
            pltpu.VMEM((nq - 1, chunk, cols), F32),
            pltpu.VMEM((nsx, chunk, cols), F32),
            pltpu.VMEM((chunk, cols), F32),
            pltpu.VMEM((nq, chunk, cols), F32),
        ]

    dma = pltpu.SemaphoreType.DMA
    first, second = pl.pallas_call(
        functools.partial(body, nsx, nsy, nsz, tx, ty),
        out_shape=[jax.ShapeDtypeStruct((tiles, width, ts), F32)] * 2,
        in_specs=[
            pl.BlockSpec(memory_space=pltpu.SMEM),
            pl.BlockSpec(memory_space=pl.ANY),
            pl.BlockSpec(memory_space=pl.ANY),
            pl.BlockSpec(memory_space=pl.ANY),
        ],
        out_specs=[pl.BlockSpec(memory_space=pltpu.VMEM)] * 2,
        scratch_shapes=[
            pltpu.VMEM((tiles * 9, ts, ts), BF16),
            pltpu.VMEM((tiles * 9, ts, ts), BF16),
            pltpu.VMEM((tiles, full + width, ts), F32),
            pltpu.VMEM((tx + 2, ty + 2, width, ts), F32),
            pltpu.VMEM((tx + 2, ty + 2, 2 * width, ts), BF16),
            pltpu.VMEM((tx + 2, ty + 2, 2, ts), F32),
            pltpu.VMEM((2, ts, 128), F32),
            pltpu.VMEM((full, full), F32),
            pltpu.VMEM((width, full + 128), F32),
        ]
        + reduce_bufs(prev + width, full)
        + reduce_bufs(width, full)
        + reduce_bufs(width, full + 128)
        + [dma((2 * tx + 2,))]
        + [dma((8,))] * 6
        + [dma((3, nq - 1))] * 2
        + [dma((3, nsx - 1))] * 2
        + [dma((3, nq - 1))] * 2,
        compiler_params=pltpu.CompilerParams(
            collective_id=0, has_side_effects=True, vmem_limit_bytes=62 * 1024 * 1024),
    )(links.reshape(-1), tiled(prior), tiled(current), tiled(site_xy))

    def untiled(x):
        return jnp.transpose(x, (1, 0, 2)).reshape(width, tx, ty, ts)

    return untiled(first), untiled(second)


def solution(mesh):
    sizes = mesh.shape
    whole = P(None, ("groups", "sx"), ("sy", "sz"), None)
    return jax.shard_map(
        functools.partial(on_device, sizes["sx"], sizes["sy"], sizes["sz"]),
        mesh=mesh,
        in_specs=(whole, whole, whole, P(None, ("groups", "sx"), ("sy", "sz"))),
        out_specs=(whole, whole),
        check_vma=False,
    )
```

```python
import functools

import jax
import jax.numpy as jnp
from jax import lax
from jax.experimental import pallas as pl
from jax.experimental.pallas import tpu as pltpu
from jax.sharding import PartitionSpec as P

GAIN = 0.0625
MESH = pl.DeviceIdType.MESH
F32 = jnp.float32
BF16 = jnp.bfloat16
HIGH = lax.Precision.HIGHEST
DIRS = [(da, db) for da in (-1, 0, 1) for db in (-1, 0, 1) if (da, db) != (0, 0)]


def dot_nn(left, right):
    return lax.dot_general(
        left, right, (((1,), (0,)), ((), ())), precision=HIGH, preferred_element_type=F32
    )


def dot_nt(left, right):
    return lax.dot_general(
        left, right, (((1,), (1,)), ((), ())), precision=HIGH, preferred_element_type=F32
    )


def dot_fast(left, right):
    return lax.dot_general(
        left, right, (((1,), (0,)), ((), ())), preferred_element_type=F32
    )


def dot_fast_nt(left, right):
    return lax.dot_general(
        left, right, (((1,), (1,)), ((), ())), preferred_element_type=F32
    )


def halves(value):
    high = value.astype(BF16)
    return high, (value - high.astype(F32)).astype(BF16)


def thirds(value):
    one = value.astype(BF16).astype(F32)
    rest = value - one
    two = rest.astype(BF16).astype(F32)
    return one, two, rest - two


def inverse_factor(gram):
    size = gram.shape[0]
    rows = lax.broadcasted_iota(jnp.int32, (size, size), 0)
    cols = lax.broadcasted_iota(jnp.int32, (size, size), 1)
    eye = jnp.where(rows == cols, 1.0, 0.0).astype(F32)
    work = jnp.concatenate([eye, gram], axis=1)
    wide = 2 * size
    rowid = lax.broadcasted_iota(jnp.int32, (size, wide), 0)
    pivots = jnp.ones((size, wide), F32)
    panel = 8
    for base in range(0, size, panel):
        cast = [
            jnp.broadcast_to(work[:, size + base + c : size + base + c + 1], (size, wide))
            for c in range(panel)
        ]
        for c in range(panel):
            k = base + c
            pivot = cast[c][k : k + 1, :]
            pivots = jnp.where(rowid == k, pivot, pivots)
            factor = jnp.where(rowid > k, cast[c] * (1.0 / pivot), 0.0)
            work = work - factor * work[k : k + 1, :]
            for d in range(c + 1, panel):
                cast[d] = cast[d] - factor * cast[d][k : k + 1, :]
    scaled = work * lax.rsqrt(pivots)
    return scaled[:, :size]


def body(
    nsx, nsy, nsz, tx, ty,
    links, prior_in, cur_in, pos_in,
    first_out, second_out,
    khi, klo, shi, slo, vpad, vbf, ppad, rowbuf, near_m, own_m, stage, image, grams, skew,
    ss_x, ss_a, ss_b, ss_z, ss_y,
    r1_x, r1_a, r1_b, r1_z, r1_y,
    r2_x, r2_a, r2_b, r2_z, r2_y,
    cur_sem, pos_sem, prior_sem, out_sem, pos_s, pos_r, v1_s, v1_r, v2_s, v2_r, pl_s, pl_r, z_s, z_r, g_s, g_r,
):
    nq = nsy * nsz
    group = lax.axis_index("groups")
    sx = lax.axis_index("sx")
    q = lax.axis_index("sy") * nsz + lax.axis_index("sz")
    prev = prior_in.shape[0]
    width = cur_in.shape[0]
    full = prev + 2 * width
    total_sites = float(tx * ty * 256 * nsx * nq)
    tiles = tx * ty

    def device(s, p):
        return (group, s, p // nsz, lax.rem(p, nsz))

    def exists(d):
        s, p = sx + d[0], q + d[1]
        return (s >= 0) & (s < nsx) & (p >= 0) & (p < nq)

    loads, prior_loads = [], []
    for t in range(tiles):
        a, b = t // ty, t % ty
        loads.append(pltpu.make_async_copy(
            pos_in.at[:, a, b], ppad.at[a + 1, b + 1], pos_sem.at[t]))
        loads.append(pltpu.make_async_copy(
            cur_in.at[:, a, b], vpad.at[a + 1, b + 1], cur_sem.at[t]))
        for h in range(prev // width):
            prior_loads.append(pltpu.make_async_copy(
                prior_in.at[pl.ds(h * width, width), a, b], stage.at[h, t],
                prior_sem.at[h, t]))
    for a in range(tx + 2):
        for b in range(ty + 2):
            if a in (0, tx + 1) or b in (0, ty + 1):
                vpad[a, b] = jnp.zeros((width, 256), F32)
                ppad[a, b] = jnp.zeros((2, 256), F32)
    for load in loads:
        load.start()
    for load in prior_loads:
        load.start()

    barrier = pltpu.get_barrier_semaphore()
    expected = jnp.int32(nq - 1 + nsx - 1)
    for d in DIRS:
        ok = exists(d)
        expected = expected + jnp.where(ok, 1, 0)

        @pl.when(ok)
        def _(d=d):
            pl.semaphore_signal(
                barrier, inc=1, device_id=device(sx + d[0], q + d[1]), device_id_type=MESH)
    for k in range(1, nq):
        pl.semaphore_signal(
            barrier, inc=1, device_id=device(sx, lax.rem(q + k, nq)), device_id_type=MESH)
    for k in range(1, nsx):
        pl.semaphore_signal(
            barrier, inc=1, device_id=device(lax.rem(sx + k, nsx), q), device_id_type=MESH)
    pl.semaphore_wait(barrier, expected)
    for load in loads:
        load.wait()

    def pick(shift, count):
        src = {-1: pl.ds(1, 1), 0: pl.ds(1, count), 1: pl.ds(count, 1)}[shift]
        dst = {-1: pl.ds(count + 1, 1), 0: pl.ds(1, count), 1: pl.ds(0, 1)}[shift]
        return src, dst

    def halo_copy(ref, i, send, recv):
        d = DIRS[i]
        (sa, da), (sb, db) = pick(d[0], tx), pick(d[1], ty)
        return pltpu.make_async_remote_copy(
            src_ref=ref.at[sa, sb], dst_ref=ref.at[da, db],
            send_sem=send.at[i], recv_sem=recv.at[i],
            device_id=device(sx + d[0], q + d[1]), device_id_type=MESH)

    def halo_start(ref, send, recv):
        for i, d in enumerate(DIRS):
            @pl.when(exists(d))
            def _(i=i):
                halo_copy(ref, i, send, recv).start()

    def halo_wait(ref, send, recv):
        for i, d in enumerate(DIRS):
            @pl.when(exists(d))
            def _(i=i):
                halo_copy(ref, i, send, recv).wait_send()

            @pl.when(exists((-d[0], -d[1])))
            def _(i=i):
                halo_copy(ref, i, send, recv).wait_recv()

    class Reduce:
        def __init__(self, which, x, a, b, z, y):
            self.w, self.x, self.a, self.b, self.z, self.y = which, x, a, b, z, y

        def plane(self, k):
            to = lax.rem(q + k, nq)
            return pltpu.make_async_remote_copy(
                src_ref=self.x.at[to], dst_ref=self.a.at[k - 1],
                send_sem=pl_s.at[self.w, k - 1], recv_sem=pl_r.at[self.w, k - 1],
                device_id=device(sx, to), device_id_type=MESH)

        def line(self, k):
            to = lax.rem(sx + k, nsx)
            return pltpu.make_async_remote_copy(
                src_ref=self.z, dst_ref=self.b.at[sx],
                send_sem=z_s.at[self.w, k - 1], recv_sem=z_r.at[self.w, k - 1],
                device_id=device(to, q), device_id_type=MESH)

        def back(self, k):
            to = lax.rem(q + k, nq)
            return pltpu.make_async_remote_copy(
                src_ref=self.y.at[q], dst_ref=self.y.at[q],
                send_sem=g_s.at[self.w, k - 1], recv_sem=g_r.at[self.w, k - 1],
                device_id=device(sx, to), device_id_type=MESH)

        def start(self):
            for k in range(1, nq):
                self.plane(k).start()

        def second(self):
            for k in range(1, nq):
                self.plane(k).wait()
            part = self.x[q]
            for k in range(1, nq):
                part = part + self.a[k - 1]
            self.z[...] = part
            for k in range(1, nsx):
                self.line(k).start()
            self.b[sx] = part

        def third(self):
            for k in range(1, nsx):
                self.line(k).wait()
            part = self.b[0]
            for k in range(1, nsx):
                part = part + self.b[k]
            self.y[q] = part * (1.0 / total_sites)
            for k in range(1, nq):
                self.back(k).start()

        def finish(self):
            for k in range(1, nq):
                self.back(k).wait()

    reduce_ss = Reduce(0, ss_x, ss_a, ss_b, ss_z, ss_y)
    reduce_1 = Reduce(1, r1_x, r1_a, r1_b, r1_z, r1_y)
    reduce_2 = Reduce(2, r2_x, r2_a, r2_b, r2_z, r2_y)

    halo_start(ppad, pos_s, pos_r)
    halo_start(vpad, v1_s, v1_r)

    def split(a, b):
        high, low = halves(vpad[a, b])
        vbf[a, b, 0:width] = high
        vbf[a, b, width : 2 * width] = low
        return high, low

    def interior(a, b):
        return (a >= 1) & (a <= tx) & (b >= 1) & (b <= ty)

    def outer(fn):
        @pl.loop(0, tx + 2)
        def _(a):
            @pl.loop(0, ty + 2)
            def _(b):
                @pl.when(jnp.logical_not(interior(a, b)))
                def _():
                    fn(a, b)

    first_rows = pl.ds(prev, width)
    cur_rows = pl.ds(prev + width, width)
    second_rows = pl.ds(prev + 2 * width, width)

    for load in prior_loads:
        load.wait()
    grams[...] = jnp.zeros_like(grams)
    skew[...] = jnp.zeros_like(skew)

    @pl.loop(0, tiles)
    def _(t):
        for h in range(prev // width):
            high, low = halves(stage[h, t])
            shi[t, h * width : (h + 1) * width] = high
            slo[t, h * width : (h + 1) * width] = low
        high, low = split(t // ty + 1, lax.rem(t, ty) + 1)
        shi[t, cur_rows] = high
        slo[t, cur_rows] = low
        shi[t, first_rows] = jnp.zeros((width, 256), BF16)
        slo[t, first_rows] = jnp.zeros((width, 256), BF16)

    group_size = 4

    @pl.loop(0, tiles // group_size)
    def _(i):
        high = [shi[i * group_size + n, 0:full] for n in range(group_size)]
        low = [slo[i * group_size + n, 0:full] for n in range(group_size)]
        grams[...] = grams[...] + sum(dot_fast_nt(h, h) for h in high)
        skew[...] = skew[...] + sum(dot_fast_nt(h, l) for h, l in zip(high, low))
    grams[...] = grams[...] + skew[...] + jnp.transpose(skew[...])
    chunk = ss_x.shape[1]
    for r in range(0, prev + width, 8):
        c, i = r // chunk, r % chunk
        row = r if r < prev else r + width
        ss_x[c, i : i + 8] = grams[row : row + 8, :]
    reduce_ss.start()

    rowbuf[...] = jnp.zeros_like(rowbuf)

    def place_terms(slot, terms):
        for k, term in enumerate(terms):
            if term is not None:
                rowbuf[slot, k : k + 1, :] = term

    def near_factors(a, b):
        x, y = ppad[a, b, 0:1, :], ppad[a, b, 1:2, :]
        xs, ys, norm = thirds(x), thirds(y), thirds(x * x + y * y)
        one = jnp.ones((1, 256), F32)
        terms = [*norm, one, one, one]
        for p in (xs, ys):
            terms += [p[0], p[0], p[1], p[1], p[0], p[2]]
        place_terms(0, terms)
        near_m[a, b] = jnp.transpose(rowbuf[0]).astype(BF16)

    def own_factors(oa, ob):
        for code in range(9):
            da, db = code // 3 - 1, code % 3 - 1
            x = ppad[oa, ob, 0:1, :] - float(da)
            y = ppad[oa, ob, 1:2, :] - float(db)
            xs, ys, norm = thirds(x), thirds(y), thirds(x * x + y * y)
            one = jnp.ones((1, 256), F32)
            terms = [one, one, one, *norm]
            for p in (xs, ys):
                terms += [-2.0 * p[n] for n in (0, 1, 0, 1, 2, 0)]
            place_terms(code, terms)
            own_m[code] = rowbuf[code].astype(BF16)

    @pl.loop(0, tiles)
    def _(t):
        near_factors(t // ty + 1, lax.rem(t, ty) + 1)

    halo_wait(ppad, pos_s, pos_r)
    outer(near_factors)
    halo_wait(vpad, v1_s, v1_r)
    outer(split)

    def make_weights(t, code):
        oa, ob = t // ty + 1, lax.rem(t, ty) + 1
        na, nb = oa + code // 3 - 1, ob + code % 3 - 1
        link = links[code, t // ty, lax.rem(t, ty)].astype(F32) * GAIN
        c4 = link * 4.0
        place = t * 9 + code
        step = 64
        for j in range(0, 256, step):
            sq = dot_fast(near_m[na, nb, j : j + step, :], own_m[code])
            sq = jnp.maximum(sq, 1e-12)
            dist = sq * lax.rsqrt(sq)
            fall = jnp.maximum(1.0 - dist, 0.0)
            two = fall * fall
            high, low = halves((two * two) * (dist * c4 + link))
            khi[place, j : j + step, :] = high
            klo[place, j : j + step, :] = low

    def apply_tile(t, rows):
        oa, ob = t // ty + 1, lax.rem(t, ty) + 1
        both, part = None, None
        for code in range(9):
            na, nb = oa + code // 3 - 1, ob + code % 3 - 1
            one = dot_fast(vbf[na, nb], khi[t * 9 + code])
            two = dot_fast(vbf[na, nb, 0:width], klo[t * 9 + code])
            both = one if both is None else both + one
            part = two if part is None else part + two
        high, low = halves(both[0:width] + both[width : 2 * width] + part)
        shi[t, rows] = high
        slo[t, rows] = low

    @pl.loop(0, tiles)
    def _(t):
        own_factors(t // ty + 1, lax.rem(t, ty) + 1)
        for code in range(9):
            make_weights(t, code)
        apply_tile(t, first_rows)

        @pl.when(t == 3)
        def _():
            reduce_ss.second()

        @pl.when(t == 7)
        def _():
            reduce_ss.third()

        @pl.when(t == 11)
        def _():
            reduce_ss.finish()

    def products(rows, extra):
        image[...] = jnp.zeros_like(image)

        @pl.loop(0, tiles // group_size)
        def _(i):
            total, mine = None, None
            for n in range(group_size):
                t = i * group_size + n
                high, low = shi[t, rows], slo[t, rows]
                both = jnp.concatenate([high, low], axis=0)
                one = dot_fast_nt(both, shi[t, 0:full])
                one = one[0:width] + one[width : 2 * width] + dot_fast_nt(high, slo[t, 0:full])
                total = one if total is None else total + one
                if extra:
                    one = dot_fast_nt(both, high)
                    one = one[0:width] + one[width : 2 * width] + dot_fast_nt(high, low)
                    mine = one if mine is None else mine + one
            image[:, 0:full] = image[:, 0:full] + total
            if extra:
                image[:, full : full + width] = image[:, full : full + width] + mine

    def reduce_now(reduce, columns):
        chunk = reduce.x.shape[1]
        for c in range(nq):
            reduce.x[c] = image[c * chunk : (c + 1) * chunk, 0:columns]
        reduce.start()
        reduce.second()
        reduce.third()
        reduce.finish()
        return jnp.concatenate([reduce.y[c] for c in range(nq)], axis=0)

    products(first_rows, False)
    chunk = ss_x.shape[1]
    grams[prev : prev + width, :] = jnp.zeros((width, full), F32)
    for r in range(0, prev + width, 8):
        c, i = r // chunk, r % chunk
        row = r if r < prev else r + width
        grams[row : row + 8, :] = ss_y[c, i : i + 8]
    lane = lax.broadcasted_iota(jnp.int32, (width, full), 1)
    inside = (lane >= prev) & (lane < prev + width)
    tlane = lax.broadcasted_iota(jnp.int32, (full, full), 1)
    grams[...] = jnp.where((tlane >= prev) & (tlane < prev + width), 0.0, grams[...])

    red = reduce_now(reduce_1, full)
    coef = jnp.where(inside, 0.0, red)
    over = dot_nn(coef, grams[...])
    gram = red[:, prev : prev + width] + dot_nt(over - 2.0 * coef, coef)
    lower = inverse_factor(gram)
    image[:, 0:full] = -dot_nn(lower, coef)
    image[:, prev : prev + width] = lower
    cross = dot_nn(lower, coef - over)
    mix_high, mix_low = halves(image[:, 0:full])
    mix = jnp.concatenate([mix_high, mix_low], axis=0)

    def mixed(mix, mix_high, high, low):
        both = dot_fast(mix, high)
        return both[0:width] + both[width : 2 * width] + dot_fast(mix_high, low)

    def first_copy(t):
        a, b = t // ty, lax.rem(t, ty)
        return pltpu.make_async_copy(
            vpad.at[a + 1, b + 1], first_out.at[:, a, b], out_sem.at[0, t])

    def second_copy(t):
        a, b = t // ty, lax.rem(t, ty)
        return pltpu.make_async_copy(
            stage.at[0, t], second_out.at[:, a, b], out_sem.at[1, t])

    @pl.loop(0, tiles // group_size)
    def _(i):
        for n in range(group_size):
            t = i * group_size + n
            a, b = t // ty + 1, lax.rem(t, ty) + 1
            fresh = mixed(mix, mix_high, shi[t, 0:full], slo[t, 0:full])
            vpad[a, b] = fresh
            high, low = halves(fresh)
            shi[t, first_rows] = high
            slo[t, first_rows] = low
            vbf[a, b, 0:width] = high
            vbf[a, b, width : 2 * width] = low

    halo_start(vpad, v2_s, v2_r)

    @pl.loop(0, tiles)
    def _(t):
        first_copy(t).start()
    rowi = lax.broadcasted_iota(jnp.int32, (width, full), 0)
    cross = jnp.where(lane == rowi + prev, 1.0, cross)
    grams[prev : prev + width, :] = cross
    grams[:, prev : prev + width] = jnp.transpose(cross)

    def inner(t):
        a, b = t // ty, lax.rem(t, ty)
        return (a >= 1) & (a < tx - 1) & (b >= 1) & (b < ty - 1)

    @pl.loop(0, tiles)
    def _(t):
        @pl.when(inner(t))
        def _():
            apply_tile(t, second_rows)
    halo_wait(vpad, v2_s, v2_r)
    outer(split)

    @pl.loop(0, tiles)
    def _(t):
        @pl.when(jnp.logical_not(inner(t)))
        def _():
            apply_tile(t, second_rows)

    products(second_rows, True)
    red = reduce_now(reduce_2, full + 128)
    coef = red[:, 0:full]
    over = dot_nn(coef, grams[...])
    gram = red[:, full : full + width] + dot_nt(over - 2.0 * coef, coef)
    lower = inverse_factor(gram)
    main_high, main_low = halves(-dot_nn(lower, coef))
    tail_high, tail_low = halves(lower)
    main = jnp.concatenate([main_high, main_low], axis=0)
    tail = jnp.concatenate([tail_high, tail_low], axis=0)

    @pl.loop(0, tiles // group_size)
    def _(i):
        for n in range(group_size):
            t = i * group_size + n
            stage[0, t] = mixed(main, main_high, shi[t, 0:full], slo[t, 0:full]) + mixed(
                tail, tail_high, shi[t, second_rows], slo[t, second_rows])
            second_copy(t).start()

    @pl.loop(0, tiles)
    def _(t):
        first_copy(t).wait()
        second_copy(t).wait()


def on_device(nsx, nsy, nsz, prior, current, site_xy, links):
    prev, tx, ty, ts = prior.shape
    width = current.shape[0]
    tiles = tx * ty
    nq = nsy * nsz
    full = prev + 2 * width

    def reduce_bufs(rows, cols):
        chunk = rows // nq
        return [
            pltpu.VMEM((nq, chunk, cols), F32),
            pltpu.VMEM((nq - 1, chunk, cols), F32),
            pltpu.VMEM((nsx, chunk, cols), F32),
            pltpu.VMEM((chunk, cols), F32),
            pltpu.VMEM((nq, chunk, cols), F32),
        ]

    dma = pltpu.SemaphoreType.DMA
    first, second = pl.pallas_call(
        functools.partial(body, nsx, nsy, nsz, tx, ty),
        out_shape=[jax.ShapeDtypeStruct(current.shape, F32)] * 2,
        in_specs=[
            pl.BlockSpec(memory_space=pltpu.SMEM),
            pl.BlockSpec(memory_space=pl.ANY),
            pl.BlockSpec(memory_space=pl.ANY),
            pl.BlockSpec(memory_space=pl.ANY),
        ],
        out_specs=[pl.BlockSpec(memory_space=pl.ANY)] * 2,
        scratch_shapes=[
            pltpu.VMEM((tiles * 9, ts, ts), BF16),
            pltpu.VMEM((tiles * 9, ts, ts), BF16),
            pltpu.VMEM((tiles, full + width, ts), BF16),
            pltpu.VMEM((tiles, full + width, ts), BF16),
            pltpu.VMEM((tx + 2, ty + 2, width, ts), F32),
            pltpu.VMEM((tx + 2, ty + 2, 2 * width, ts), BF16),
            pltpu.VMEM((tx + 2, ty + 2, 2, ts), F32),
            pltpu.VMEM((9, 32, ts), F32),
            pltpu.VMEM((tx + 2, ty + 2, ts, 32), BF16),
            pltpu.VMEM((9, 32, ts), BF16),
            pltpu.VMEM((prev // width, tiles, width, ts), F32),
            pltpu.VMEM((width, full + 128), F32),
            pltpu.VMEM((full, full), F32),
            pltpu.VMEM((full, full), F32),
        ]
        + reduce_bufs(prev + width, full)
        + reduce_bufs(width, full)
        + reduce_bufs(width, full + 128)
        + [dma((tiles,))] * 2
        + [dma((prev // width, tiles)), dma((2, tiles))]
        + [dma((8,))] * 6
        + [dma((3, nq - 1))] * 2
        + [dma((3, nsx - 1))] * 2
        + [dma((3, nq - 1))] * 2,
        compiler_params=pltpu.CompilerParams(
            collective_id=0, has_side_effects=True, vmem_limit_bytes=62 * 1024 * 1024),
    )(links, prior, current, site_xy)
    return first, second


def solution(mesh):
    sizes = mesh.shape
    whole = P(None, ("groups", "sx"), ("sy", "sz"), None)
    return jax.shard_map(
        functools.partial(on_device, sizes["sx"], sizes["sy"], sizes["sz"]),
        mesh=mesh,
        in_specs=(whole, whole, whole, P(None, ("groups", "sx"), ("sy", "sz"))),
        out_specs=(whole, whole),
        check_vma=False,
    )
```

```python
import functools

import jax
import jax.numpy as jnp
from jax import lax
from jax.experimental import pallas as pl
from jax.experimental.pallas import tpu as pltpu
from jax.sharding import PartitionSpec as P

GAIN = 0.0625
MESH = pl.DeviceIdType.MESH
F32 = jnp.float32
BF16 = jnp.bfloat16
HIGH = lax.Precision.HIGHEST
DIRS = [(da, db) for da in (-1, 0, 1) for db in (-1, 0, 1) if (da, db) != (0, 0)]


def dot_nn(left, right):
    return lax.dot_general(
        left, right, (((1,), (0,)), ((), ())), precision=HIGH, preferred_element_type=F32
    )


def dot_nt(left, right):
    return lax.dot_general(
        left, right, (((1,), (1,)), ((), ())), precision=HIGH, preferred_element_type=F32
    )


def dot_fast(left, right):
    return lax.dot_general(
        left, right, (((1,), (0,)), ((), ())), preferred_element_type=F32
    )


def dot_fast_nt(left, right):
    return lax.dot_general(
        left, right, (((1,), (1,)), ((), ())), preferred_element_type=F32
    )


def halves(value):
    high = value.astype(BF16)
    return high, (value - high.astype(F32)).astype(BF16)


def thirds(value):
    one = value.astype(BF16).astype(F32)
    rest = value - one
    two = rest.astype(BF16).astype(F32)
    return one, two, rest - two


def inverse_factor(gram):
    size = gram.shape[0]
    rows = lax.broadcasted_iota(jnp.int32, (size, size), 0)
    cols = lax.broadcasted_iota(jnp.int32, (size, size), 1)
    eye = jnp.where(rows == cols, 1.0, 0.0).astype(F32)
    work = jnp.concatenate([eye, gram], axis=1)
    wide = 2 * size
    rowid = lax.broadcasted_iota(jnp.int32, (size, wide), 0)
    pivots = jnp.ones((size, wide), F32)
    panel = 8
    for base in range(0, size, panel):
        cast = [
            jnp.broadcast_to(work[:, size + base + c : size + base + c + 1], (size, wide))
            for c in range(panel)
        ]
        for c in range(panel):
            k = base + c
            pivot = cast[c][k : k + 1, :]
            pivots = jnp.where(rowid == k, pivot, pivots)
            factor = jnp.where(rowid > k, cast[c] * (1.0 / pivot), 0.0)
            work = work - factor * work[k : k + 1, :]
            for d in range(c + 1, panel):
                cast[d] = cast[d] - factor * cast[d][k : k + 1, :]
    scaled = work * lax.rsqrt(pivots)
    return scaled[:, :size]


def is_flat(nsx, nq):
    return nsx * nq <= 16


def body(
    nsx, nsy, nsz, tx, ty,
    links, prior_in, cur_in, pos_in,
    first_out, second_out,
    khi, klo, shi, slo, vpad, vbf, ppad, rowbuf, near_m, own_m, stage, image, grams, skew,
    ss_x, ss_a, ss_b, ss_z, ss_y,
    r1_x, r1_a, r1_b, r1_z, r1_y,
    r2_x, r2_a, r2_b, r2_z, r2_y,
    cur_sem, pos_sem, prior_sem, out_sem, pos_s, pos_r, v1_s, v1_r, v2_s, v2_r, pl_s, pl_r, z_s, z_r, g_s, g_r,
):
    nq = nsy * nsz
    count = nsx * nq
    flat = is_flat(nsx, nq)
    group = lax.axis_index("groups")
    sx = lax.axis_index("sx")
    q = lax.axis_index("sy") * nsz + lax.axis_index("sz")
    prev = prior_in.shape[0]
    width = cur_in.shape[0]
    full = prev + 2 * width
    total_sites = float(tx * ty * 256 * nsx * nq)
    tiles = tx * ty

    def device(s, p):
        return (group, s, p // nsz, lax.rem(p, nsz))

    def exists(d):
        s, p = sx + d[0], q + d[1]
        return (s >= 0) & (s < nsx) & (p >= 0) & (p < nq)

    loads, prior_loads = [], []
    for t in range(tiles):
        a, b = t // ty, t % ty
        loads.append(pltpu.make_async_copy(
            pos_in.at[:, a, b], ppad.at[a + 1, b + 1], pos_sem.at[t]))
        loads.append(pltpu.make_async_copy(
            cur_in.at[:, a, b], vpad.at[a + 1, b + 1], cur_sem.at[t]))
        for h in range(prev // width):
            prior_loads.append(pltpu.make_async_copy(
                prior_in.at[pl.ds(h * width, width), a, b], stage.at[h, t],
                prior_sem.at[h, t]))
    for a in range(tx + 2):
        for b in range(ty + 2):
            if a in (0, tx + 1) or b in (0, ty + 1):
                vpad[a, b] = jnp.zeros((width, 256), F32)
                ppad[a, b] = jnp.zeros((2, 256), F32)
    for load in loads:
        load.start()
    for load in prior_loads:
        load.start()

    barrier = pltpu.get_barrier_semaphore()
    expected = jnp.int32(count - 1 if flat else nq - 1 + nsx - 1)
    for d in DIRS:
        ok = exists(d)
        expected = expected + jnp.where(ok, 1, 0)

        @pl.when(ok)
        def _(d=d):
            pl.semaphore_signal(
                barrier, inc=1, device_id=device(sx + d[0], q + d[1]), device_id_type=MESH)
    if flat:
        for k in range(1, count):
            to = lax.rem(sx * nq + q + k, count)
            pl.semaphore_signal(
                barrier, inc=1, device_id=device(to // nq, lax.rem(to, nq)), device_id_type=MESH)
    else:
        for k in range(1, nq):
            pl.semaphore_signal(
                barrier, inc=1, device_id=device(sx, lax.rem(q + k, nq)), device_id_type=MESH)
        for k in range(1, nsx):
            pl.semaphore_signal(
                barrier, inc=1, device_id=device(lax.rem(sx + k, nsx), q), device_id_type=MESH)
    pl.semaphore_wait(barrier, expected)
    for load in loads[0::2]:
        load.wait()

    def pick(shift, count):
        src = {-1: pl.ds(1, 1), 0: pl.ds(1, count), 1: pl.ds(count, 1)}[shift]
        dst = {-1: pl.ds(count + 1, 1), 0: pl.ds(1, count), 1: pl.ds(0, 1)}[shift]
        return src, dst

    def halo_copy(ref, i, send, recv):
        d = DIRS[i]
        (sa, da), (sb, db) = pick(d[0], tx), pick(d[1], ty)
        return pltpu.make_async_remote_copy(
            src_ref=ref.at[sa, sb], dst_ref=ref.at[da, db],
            send_sem=send.at[i], recv_sem=recv.at[i],
            device_id=device(sx + d[0], q + d[1]), device_id_type=MESH)

    def halo_start(ref, send, recv):
        for i, d in enumerate(DIRS):
            @pl.when(exists(d))
            def _(i=i):
                halo_copy(ref, i, send, recv).start()

    def halo_wait(ref, send, recv):
        for i, d in enumerate(DIRS):
            @pl.when(exists(d))
            def _(i=i):
                halo_copy(ref, i, send, recv).wait_send()

            @pl.when(exists((-d[0], -d[1])))
            def _(i=i):
                halo_copy(ref, i, send, recv).wait_recv()

    me = sx * nq + q

    def member(p):
        return device(p // nq, lax.rem(p, nq))

    class ReduceFlat:
        def __init__(self, which, x, a, b, z, y):
            self.w, self.x, self.a, self.y = which, x, a, y

        def scatter(self, k):
            to = lax.rem(me + k, count)
            return pltpu.make_async_remote_copy(
                src_ref=self.x.at[to], dst_ref=self.a.at[k - 1],
                send_sem=pl_s.at[self.w, k - 1], recv_sem=pl_r.at[self.w, k - 1],
                device_id=member(to), device_id_type=MESH)

        def back(self, k):
            to = lax.rem(me + k, count)
            return pltpu.make_async_remote_copy(
                src_ref=self.y.at[me], dst_ref=self.y.at[me],
                send_sem=g_s.at[self.w, k - 1], recv_sem=g_r.at[self.w, k - 1],
                device_id=member(to), device_id_type=MESH)

        def start(self):
            for k in range(1, count):
                self.scatter(k).start()

        def second(self):
            part = self.x[me]
            for k in range(1, count):
                self.scatter(k).wait_recv()
            for k in range(1, count):
                part = part + self.a[k - 1]
            self.y[me] = part * (1.0 / total_sites)
            for k in range(1, count):
                self.back(k).start()

        def third(self):
            for k in range(1, count):
                self.scatter(k).wait_send()

        def finish(self):
            for k in range(1, count):
                self.back(k).wait()

    class Reduce:
        def __init__(self, which, x, a, b, z, y):
            self.w, self.x, self.a, self.b, self.z, self.y = which, x, a, b, z, y

        def plane(self, k):
            to = lax.rem(q + k, nq)
            return pltpu.make_async_remote_copy(
                src_ref=self.x.at[to], dst_ref=self.a.at[k - 1],
                send_sem=pl_s.at[self.w, k - 1], recv_sem=pl_r.at[self.w, k - 1],
                device_id=device(sx, to), device_id_type=MESH)

        def line(self, k):
            to = lax.rem(sx + k, nsx)
            return pltpu.make_async_remote_copy(
                src_ref=self.z, dst_ref=self.b.at[sx],
                send_sem=z_s.at[self.w, k - 1], recv_sem=z_r.at[self.w, k - 1],
                device_id=device(to, q), device_id_type=MESH)

        def back(self, k):
            to = lax.rem(q + k, nq)
            return pltpu.make_async_remote_copy(
                src_ref=self.y.at[q], dst_ref=self.y.at[q],
                send_sem=g_s.at[self.w, k - 1], recv_sem=g_r.at[self.w, k - 1],
                device_id=device(sx, to), device_id_type=MESH)

        def start(self):
            for k in range(1, nq):
                self.plane(k).start()

        def second(self):
            for k in range(1, nq):
                self.plane(k).wait()
            part = self.x[q]
            for k in range(1, nq):
                part = part + self.a[k - 1]
            self.z[...] = part
            for k in range(1, nsx):
                self.line(k).start()
            self.b[sx] = part

        def third(self):
            for k in range(1, nsx):
                self.line(k).wait()
            part = self.b[0]
            for k in range(1, nsx):
                part = part + self.b[k]
            self.y[q] = part * (1.0 / total_sites)
            for k in range(1, nq):
                self.back(k).start()

        def finish(self):
            for k in range(1, nq):
                self.back(k).wait()

    reduce_ss = (ReduceFlat if flat else Reduce)(0, ss_x, ss_a, ss_b, ss_z, ss_y)
    reduce_1 = (ReduceFlat if flat else Reduce)(1, r1_x, r1_a, r1_b, r1_z, r1_y)
    reduce_2 = (ReduceFlat if flat else Reduce)(2, r2_x, r2_a, r2_b, r2_z, r2_y)

    halo_start(ppad, pos_s, pos_r)
    for load in loads[1::2]:
        load.wait()
    halo_start(vpad, v1_s, v1_r)

    def split(a, b):
        high, low = halves(vpad[a, b])
        vbf[a, b, 0:width] = high
        vbf[a, b, width : 2 * width] = low
        return high, low

    def interior(a, b):
        return (a >= 1) & (a <= tx) & (b >= 1) & (b <= ty)

    def split_halo():
        for b in range(ty + 2):
            split(0, b)
            split(tx + 1, b)
        for a in range(1, tx + 1):
            split(a, 0)
            split(a, ty + 1)

    first_rows = pl.ds(prev, width)
    cur_rows = pl.ds(prev + width, width)
    second_rows = pl.ds(prev + 2 * width, width)

    @pl.loop(0, tiles)
    def _(t):
        high, low = split(t // ty + 1, lax.rem(t, ty) + 1)
        shi[t, cur_rows] = high
        slo[t, cur_rows] = low
        shi[t, first_rows] = jnp.zeros((width, 256), BF16)
        slo[t, first_rows] = jnp.zeros((width, 256), BF16)

    rowbuf[...] = jnp.zeros_like(rowbuf)
    halo_wait(ppad, pos_s, pos_r)

    def place_terms(slot, terms):
        for k, term in enumerate(terms):
            if term is not None:
                rowbuf[slot, k : k + 1, :] = term

    def near_factors(a, b):
        x, y = ppad[a, b, 0:1, :], ppad[a, b, 1:2, :]
        xs, ys, norm = thirds(x), thirds(y), thirds(x * x + y * y)
        one = jnp.ones((1, 256), F32)
        terms = [*norm, one, one, one]
        for p in (xs, ys):
            terms += [p[0], p[0], p[1], p[1], p[0], p[2]]
        place_terms(b, terms)
        near_m[a, b] = jnp.transpose(rowbuf[b]).astype(BF16)

    def own_factors(oa, ob):
        for code in range(9):
            da, db = code // 3 - 1, code % 3 - 1
            x = ppad[oa, ob, 0:1, :] - float(da)
            y = ppad[oa, ob, 1:2, :] - float(db)
            xs, ys, norm = thirds(x), thirds(y), thirds(x * x + y * y)
            one = jnp.ones((1, 256), F32)
            terms = [one, one, one, *norm]
            for p in (xs, ys):
                terms += [-2.0 * p[n] for n in (0, 1, 0, 1, 2, 0)]
            place_terms(code, terms)
            own_m[code] = rowbuf[code].astype(BF16)

    @pl.loop(0, tx + 2)
    def _(a):
        for b in range(ty + 2):
            near_factors(a, b)

    for load in prior_loads:
        load.wait()
    grams[...] = jnp.zeros_like(grams)
    skew[...] = jnp.zeros_like(skew)

    @pl.loop(0, tiles)
    def _(t):
        for h in range(prev // width):
            high, low = halves(stage[h, t])
            shi[t, h * width : (h + 1) * width] = high
            slo[t, h * width : (h + 1) * width] = low

    group_size = 4

    @pl.loop(0, tiles // group_size)
    def _(i):
        high = [shi[i * group_size + n, 0:full] for n in range(group_size)]
        low = [slo[i * group_size + n, 0:full] for n in range(group_size)]
        grams[...] = grams[...] + sum(dot_fast_nt(h, h) for h in high)
        skew[...] = skew[...] + sum(dot_fast_nt(h, l) for h, l in zip(high, low))
    grams[...] = grams[...] + skew[...] + jnp.transpose(skew[...])
    chunk = ss_x.shape[1]
    for r in range(0, prev + width, 4):
        c, i = r // chunk, r % chunk
        row = r if r < prev else r + width
        ss_x[c, i : i + 4] = grams[row : row + 4, :]
    reduce_ss.start()

    halo_wait(vpad, v1_s, v1_r)
    split_halo()

    def make_weights(t, code):
        oa, ob = t // ty + 1, lax.rem(t, ty) + 1
        na, nb = oa + code // 3 - 1, ob + code % 3 - 1
        link = links[code, t // ty, lax.rem(t, ty)].astype(F32) * GAIN
        c4 = link * 4.0
        place = t * 9 + code
        step = 64
        for j in range(0, 256, step):
            sq = dot_fast(near_m[na, nb, j : j + step, :], own_m[code])
            sq = jnp.maximum(sq, 1e-12)
            dist = sq * lax.rsqrt(sq)
            fall = jnp.maximum(1.0 - dist, 0.0)
            two = fall * fall
            high, low = halves((two * two) * (dist * c4 + link))
            khi[place, j : j + step, :] = high
            klo[place, j : j + step, :] = low

    def apply_tile(t, rows):
        oa, ob = t // ty + 1, lax.rem(t, ty) + 1
        both, part = None, None
        for code in range(9):
            na, nb = oa + code // 3 - 1, ob + code % 3 - 1
            one = dot_fast(vbf[na, nb], khi[t * 9 + code])
            two = dot_fast(vbf[na, nb, 0:width], klo[t * 9 + code])
            both = one if both is None else both + one
            part = two if part is None else part + two
        high, low = halves(both[0:width] + both[width : 2 * width] + part)
        shi[t, rows] = high
        slo[t, rows] = low

    @pl.loop(0, tiles)
    def _(t):
        own_factors(t // ty + 1, lax.rem(t, ty) + 1)
        for code in range(9):
            make_weights(t, code)
        apply_tile(t, first_rows)

        @pl.when(t == 3)
        def _():
            reduce_ss.second()

        @pl.when(t == 7)
        def _():
            reduce_ss.third()

        @pl.when(t == 11)
        def _():
            reduce_ss.finish()

    def products(rows, extra):
        image[...] = jnp.zeros_like(image)

        @pl.loop(0, tiles // group_size)
        def _(i):
            total, mine = None, None
            for n in range(group_size):
                t = i * group_size + n
                high, low = shi[t, rows], slo[t, rows]
                both = jnp.concatenate([high, low], axis=0)
                one = dot_fast_nt(both, shi[t, 0:full])
                one = one[0:width] + one[width : 2 * width] + dot_fast_nt(high, slo[t, 0:full])
                total = one if total is None else total + one
                if extra:
                    one = dot_fast_nt(both, high)
                    one = one[0:width] + one[width : 2 * width] + dot_fast_nt(high, low)
                    mine = one if mine is None else mine + one
            image[:, 0:full] = image[:, 0:full] + total
            if extra:
                image[:, full : full + width] = image[:, full : full + width] + mine

    def reduce_now(reduce, columns):
        chunk = reduce.x.shape[1]
        chunks = reduce.x.shape[0]
        for c in range(chunks):
            reduce.x[c] = image[c * chunk : (c + 1) * chunk, 0:columns]
        reduce.start()
        reduce.second()
        reduce.third()
        reduce.finish()
        for c in range(chunks):
            image[c * chunk : (c + 1) * chunk, 0:columns] = reduce.y[c]
        return image[:, 0:columns]

    products(first_rows, False)
    chunk = ss_x.shape[1]
    grams[prev : prev + width, :] = jnp.zeros((width, full), F32)
    for r in range(0, prev + width, 4):
        c, i = r // chunk, r % chunk
        row = r if r < prev else r + width
        grams[row : row + 4, :] = ss_y[c, i : i + 4]
    lane = lax.broadcasted_iota(jnp.int32, (width, full), 1)
    inside = (lane >= prev) & (lane < prev + width)
    tlane = lax.broadcasted_iota(jnp.int32, (full, full), 1)
    grams[...] = jnp.where((tlane >= prev) & (tlane < prev + width), 0.0, grams[...])

    red = reduce_now(reduce_1, full)
    coef = jnp.where(inside, 0.0, red)
    over = dot_nn(coef, grams[...])
    gram = red[:, prev : prev + width] + dot_nt(over - 2.0 * coef, coef)
    lower = inverse_factor(gram)
    image[:, 0:full] = -dot_nn(lower, coef)
    image[:, prev : prev + width] = lower
    cross = dot_nn(lower, coef - over)
    mix_high, mix_low = halves(image[:, 0:full])
    mix = jnp.concatenate([mix_high, mix_low], axis=0)

    def mixed(mix, mix_high, high, low):
        both = dot_fast(mix, high)
        return both[0:width] + both[width : 2 * width] + dot_fast(mix_high, low)

    def first_copy(t):
        a, b = t // ty, lax.rem(t, ty)
        return pltpu.make_async_copy(
            vpad.at[a + 1, b + 1], first_out.at[:, a, b], out_sem.at[0, t])

    def second_copy(t):
        a, b = t // ty, lax.rem(t, ty)
        return pltpu.make_async_copy(
            stage.at[0, t], second_out.at[:, a, b], out_sem.at[1, t])

    @pl.loop(0, tiles // group_size)
    def _(i):
        for n in range(group_size):
            t = i * group_size + n
            a, b = t // ty + 1, lax.rem(t, ty) + 1
            fresh = mixed(mix, mix_high, shi[t, 0:full], slo[t, 0:full])
            vpad[a, b] = fresh
            high, low = halves(fresh)
            shi[t, first_rows] = high
            slo[t, first_rows] = low
            vbf[a, b, 0:width] = high
            vbf[a, b, width : 2 * width] = low

    halo_start(vpad, v2_s, v2_r)

    @pl.loop(0, tiles)
    def _(t):
        first_copy(t).start()
    rowi = lax.broadcasted_iota(jnp.int32, (width, full), 0)
    cross = jnp.where(lane == rowi + prev, 1.0, cross)
    grams[prev : prev + width, :] = cross
    grams[:, prev : prev + width] = jnp.transpose(cross)

    def inner(t):
        a, b = t // ty, lax.rem(t, ty)
        return (a >= 1) & (a < tx - 1) & (b >= 1) & (b < ty - 1)

    @pl.loop(0, tiles)
    def _(t):
        @pl.when(inner(t))
        def _():
            apply_tile(t, second_rows)
    halo_wait(vpad, v2_s, v2_r)
    split_halo()

    @pl.loop(0, tiles)
    def _(t):
        @pl.when(jnp.logical_not(inner(t)))
        def _():
            apply_tile(t, second_rows)

    products(second_rows, True)
    red = reduce_now(reduce_2, full + 128)
    coef = red[:, 0:full]
    over = dot_nn(coef, grams[...])
    gram = red[:, full : full + width] + dot_nt(over - 2.0 * coef, coef)
    lower = inverse_factor(gram)
    main_high, main_low = halves(-dot_nn(lower, coef))
    tail_high, tail_low = halves(lower)
    main = jnp.concatenate([main_high, main_low], axis=0)
    tail = jnp.concatenate([tail_high, tail_low], axis=0)

    @pl.loop(0, tiles // group_size)
    def _(i):
        for n in range(group_size):
            t = i * group_size + n
            stage[0, t] = mixed(main, main_high, shi[t, 0:full], slo[t, 0:full]) + mixed(
                tail, tail_high, shi[t, second_rows], slo[t, second_rows])
            second_copy(t).start()

    @pl.loop(0, tiles)
    def _(t):
        first_copy(t).wait()
        second_copy(t).wait()


def on_device(nsx, nsy, nsz, prior, current, site_xy, links):
    prev, tx, ty, ts = prior.shape
    width = current.shape[0]
    tiles = tx * ty
    nq = nsy * nsz
    full = prev + 2 * width

    def reduce_bufs(rows, cols):
        if is_flat(nsx, nq):
            count = nsx * nq
            chunk = rows // count
            return [
                pltpu.VMEM((count, chunk, cols), F32),
                pltpu.VMEM((count - 1, chunk, cols), F32),
                pltpu.VMEM((8, 128), F32),
                pltpu.VMEM((8, 128), F32),
                pltpu.VMEM((count, chunk, cols), F32),
            ]
        chunk = rows // nq
        return [
            pltpu.VMEM((nq, chunk, cols), F32),
            pltpu.VMEM((nq - 1, chunk, cols), F32),
            pltpu.VMEM((nsx, chunk, cols), F32),
            pltpu.VMEM((chunk, cols), F32),
            pltpu.VMEM((nq, chunk, cols), F32),
        ]

    dma = pltpu.SemaphoreType.DMA
    peers = (nsx * nq if is_flat(nsx, nq) else nq) - 1
    first, second = pl.pallas_call(
        functools.partial(body, nsx, nsy, nsz, tx, ty),
        out_shape=[jax.ShapeDtypeStruct(current.shape, F32)] * 2,
        in_specs=[
            pl.BlockSpec(memory_space=pltpu.SMEM),
            pl.BlockSpec(memory_space=pl.ANY),
            pl.BlockSpec(memory_space=pl.ANY),
            pl.BlockSpec(memory_space=pl.ANY),
        ],
        out_specs=[pl.BlockSpec(memory_space=pl.ANY)] * 2,
        scratch_shapes=[
            pltpu.VMEM((tiles * 9, ts, ts), BF16),
            pltpu.VMEM((tiles * 9, ts, ts), BF16),
            pltpu.VMEM((tiles, full + width, ts), BF16),
            pltpu.VMEM((tiles, full + width, ts), BF16),
            pltpu.VMEM((tx + 2, ty + 2, width, ts), F32),
            pltpu.VMEM((tx + 2, ty + 2, 2 * width, ts), BF16),
            pltpu.VMEM((tx + 2, ty + 2, 2, ts), F32),
            pltpu.VMEM((9, 32, ts), F32),
            pltpu.VMEM((tx + 2, ty + 2, ts, 32), BF16),
            pltpu.VMEM((9, 32, ts), BF16),
            pltpu.VMEM((prev // width, tiles, width, ts), F32),
            pltpu.VMEM((width, full + 128), F32),
            pltpu.VMEM((full, full), F32),
            pltpu.VMEM((full, full), F32),
        ]
        + reduce_bufs(prev + width, full)
        + reduce_bufs(width, full)
        + reduce_bufs(width, full + 128)
        + [dma((tiles,))] * 2
        + [dma((prev // width, tiles)), dma((2, tiles))]
        + [dma((8,))] * 6
        + [dma((3, peers))] * 2
        + [dma((3, nsx - 1))] * 2
        + [dma((3, peers))] * 2,
        compiler_params=pltpu.CompilerParams(
            collective_id=0, has_side_effects=True, vmem_limit_bytes=62 * 1024 * 1024),
    )(links, prior, current, site_xy)
    return first, second


def solution(mesh):
    sizes = mesh.shape
    whole = P(None, ("groups", "sx"), ("sy", "sz"), None)
    return jax.shard_map(
        functools.partial(on_device, sizes["sx"], sizes["sy"], sizes["sz"]),
        mesh=mesh,
        in_specs=(whole, whole, whole, P(None, ("groups", "sx"), ("sy", "sz"))),
        out_specs=(whole, whole),
        check_vma=False,
    )
```

```python
import functools

import jax
import jax.numpy as jnp
from jax import lax
from jax.experimental import pallas as pl
from jax.experimental.pallas import tpu as pltpu
from jax.sharding import PartitionSpec as P

GAIN = 0.0625
MESH = pl.DeviceIdType.MESH
F32 = jnp.float32
BF16 = jnp.bfloat16
HIGH = lax.Precision.HIGHEST
DIRS = [(da, db) for da in (-1, 0, 1) for db in (-1, 0, 1) if (da, db) != (0, 0)]


def dot_nn(left, right):
    return lax.dot_general(
        left, right, (((1,), (0,)), ((), ())), precision=HIGH, preferred_element_type=F32
    )


def dot_nt(left, right):
    return lax.dot_general(
        left, right, (((1,), (1,)), ((), ())), precision=HIGH, preferred_element_type=F32
    )


def dot_fast(left, right):
    return lax.dot_general(
        left, right, (((1,), (0,)), ((), ())), preferred_element_type=F32
    )


def dot_fast_nt(left, right):
    return lax.dot_general(
        left, right, (((1,), (1,)), ((), ())), preferred_element_type=F32
    )


def halves(value):
    high = value.astype(BF16)
    return high, (value - high.astype(F32)).astype(BF16)


def thirds(value):
    one = value.astype(BF16).astype(F32)
    rest = value - one
    two = rest.astype(BF16).astype(F32)
    return one, two, rest - two


def inverse_factor(gram):
    size = gram.shape[0]
    rows = lax.broadcasted_iota(jnp.int32, (size, size), 0)
    cols = lax.broadcasted_iota(jnp.int32, (size, size), 1)
    eye = jnp.where(rows == cols, 1.0, 0.0).astype(F32)
    work = jnp.concatenate([eye, gram], axis=1)
    wide = 2 * size
    rowid = lax.broadcasted_iota(jnp.int32, (size, wide), 0)
    pivots = jnp.ones((size, wide), F32)
    panel = 8
    for base in range(0, size, panel):
        cast = [
            jnp.broadcast_to(work[:, size + base + c : size + base + c + 1], (size, wide))
            for c in range(panel)
        ]
        for c in range(panel):
            k = base + c
            pivot = cast[c][k : k + 1, :]
            pivots = jnp.where(rowid == k, pivot, pivots)
            factor = jnp.where(rowid > k, cast[c] * (1.0 / pivot), 0.0)
            work = work - factor * work[k : k + 1, :]
            for d in range(c + 1, panel):
                cast[d] = cast[d] - factor * cast[d][k : k + 1, :]
    scaled = work * lax.rsqrt(pivots)
    return scaled[:, :size]


def is_flat(nsx, nq):
    return nsx * nq <= 4


def body(
    nsx, nsy, nsz, tx, ty,
    links, prior_in, cur_in, pos_in,
    first_out, second_out,
    khi, klo, shi, slo, vpad, vbf, ppad, rowbuf, near_m, own_m, stage, image, grams, skew,
    ss_x, ss_a, ss_b, ss_z, ss_y,
    r1_x, r1_a, r1_b, r1_z, r1_y,
    r2_x, r2_a, r2_b, r2_z, r2_y,
    cur_sem, pos_sem, prior_sem, out_sem, pos_s, pos_r, v1_s, v1_r, v2_s, v2_r, pl_s, pl_r, z_s, z_r, g_s, g_r,
):
    nq = nsy * nsz
    count = nsx * nq
    flat = is_flat(nsx, nq)
    group = lax.axis_index("groups")
    sx = lax.axis_index("sx")
    q = lax.axis_index("sy") * nsz + lax.axis_index("sz")
    prev = prior_in.shape[0]
    width = cur_in.shape[0]
    full = prev + 2 * width
    total_sites = float(tx * ty * 256 * nsx * nq)
    tiles = tx * ty

    def device(s, p):
        return (group, s, p // nsz, lax.rem(p, nsz))

    def exists(d):
        s, p = sx + d[0], q + d[1]
        return (s >= 0) & (s < nsx) & (p >= 0) & (p < nq)

    loads, prior_loads = [], []
    for t in range(tiles):
        a, b = t // ty, t % ty
        loads.append(pltpu.make_async_copy(
            pos_in.at[:, a, b], ppad.at[a + 1, b + 1], pos_sem.at[t]))
        loads.append(pltpu.make_async_copy(
            cur_in.at[:, a, b], vpad.at[a + 1, b + 1], cur_sem.at[t]))
        for h in range(prev // width):
            prior_loads.append(pltpu.make_async_copy(
                prior_in.at[pl.ds(h * width, width), a, b], stage.at[h, t],
                prior_sem.at[h, t]))
    for a in range(tx + 2):
        for b in range(ty + 2):
            if a in (0, tx + 1) or b in (0, ty + 1):
                vpad[a, b] = jnp.zeros((width, 256), F32)
                ppad[a, b] = jnp.zeros((2, 256), F32)
    for load in loads:
        load.start()
    for load in prior_loads:
        load.start()

    barrier = pltpu.get_barrier_semaphore()
    expected = jnp.int32(count - 1 if flat else nq - 1 + nsx - 1)
    for d in DIRS:
        ok = exists(d)
        expected = expected + jnp.where(ok, 1, 0)

        @pl.when(ok)
        def _(d=d):
            pl.semaphore_signal(
                barrier, inc=1, device_id=device(sx + d[0], q + d[1]), device_id_type=MESH)
    if flat:
        for k in range(1, count):
            to = lax.rem(sx * nq + q + k, count)
            pl.semaphore_signal(
                barrier, inc=1, device_id=device(to // nq, lax.rem(to, nq)), device_id_type=MESH)
    else:
        for k in range(1, nq):
            pl.semaphore_signal(
                barrier, inc=1, device_id=device(sx, lax.rem(q + k, nq)), device_id_type=MESH)
        for k in range(1, nsx):
            pl.semaphore_signal(
                barrier, inc=1, device_id=device(lax.rem(sx + k, nsx), q), device_id_type=MESH)
    pl.semaphore_wait(barrier, expected)
    for load in loads[0::2]:
        load.wait()

    def pick(shift, count):
        src = {-1: pl.ds(1, 1), 0: pl.ds(1, count), 1: pl.ds(count, 1)}[shift]
        dst = {-1: pl.ds(count + 1, 1), 0: pl.ds(1, count), 1: pl.ds(0, 1)}[shift]
        return src, dst

    def halo_copy(ref, i, send, recv):
        d = DIRS[i]
        (sa, da), (sb, db) = pick(d[0], tx), pick(d[1], ty)
        return pltpu.make_async_remote_copy(
            src_ref=ref.at[sa, sb], dst_ref=ref.at[da, db],
            send_sem=send.at[i], recv_sem=recv.at[i],
            device_id=device(sx + d[0], q + d[1]), device_id_type=MESH)

    def halo_start(ref, send, recv):
        for i, d in enumerate(DIRS):
            @pl.when(exists(d))
            def _(i=i):
                halo_copy(ref, i, send, recv).start()

    def halo_wait(ref, send, recv):
        for i, d in enumerate(DIRS):
            @pl.when(exists(d))
            def _(i=i):
                halo_copy(ref, i, send, recv).wait_send()

            @pl.when(exists((-d[0], -d[1])))
            def _(i=i):
                halo_copy(ref, i, send, recv).wait_recv()

    me = sx * nq + q

    def member(p):
        return device(p // nq, lax.rem(p, nq))

    class ReduceFlat:
        def __init__(self, which, x, a, b, z, y):
            self.w, self.x, self.a, self.y = which, x, a, y

        def scatter(self, k):
            to = lax.rem(me + k, count)
            return pltpu.make_async_remote_copy(
                src_ref=self.x.at[to], dst_ref=self.a.at[k - 1],
                send_sem=pl_s.at[self.w, k - 1], recv_sem=pl_r.at[self.w, k - 1],
                device_id=member(to), device_id_type=MESH)

        def back(self, k):
            to = lax.rem(me + k, count)
            return pltpu.make_async_remote_copy(
                src_ref=self.y.at[me], dst_ref=self.y.at[me],
                send_sem=g_s.at[self.w, k - 1], recv_sem=g_r.at[self.w, k - 1],
                device_id=member(to), device_id_type=MESH)

        def start(self):
            for k in range(1, count):
                self.scatter(k).start()

        def second(self):
            part = self.x[me]
            for k in range(1, count):
                self.scatter(k).wait_recv()
            for k in range(1, count):
                part = part + self.a[k - 1]
            self.y[me] = part * (1.0 / total_sites)
            for k in range(1, count):
                self.back(k).start()

        def third(self):
            for k in range(1, count):
                self.scatter(k).wait_send()

        def finish(self):
            for k in range(1, count):
                self.back(k).wait()

    class Reduce:
        def __init__(self, which, x, a, b, z, y):
            self.w, self.x, self.a, self.b, self.z, self.y = which, x, a, b, z, y

        def plane(self, k):
            to = lax.rem(q + k, nq)
            return pltpu.make_async_remote_copy(
                src_ref=self.x.at[to], dst_ref=self.a.at[k - 1],
                send_sem=pl_s.at[self.w, k - 1], recv_sem=pl_r.at[self.w, k - 1],
                device_id=device(sx, to), device_id_type=MESH)

        def line(self, k):
            to = lax.rem(sx + k, nsx)
            return pltpu.make_async_remote_copy(
                src_ref=self.z, dst_ref=self.b.at[sx],
                send_sem=z_s.at[self.w, k - 1], recv_sem=z_r.at[self.w, k - 1],
                device_id=device(to, q), device_id_type=MESH)

        def back(self, k):
            to = lax.rem(q + k, nq)
            return pltpu.make_async_remote_copy(
                src_ref=self.y.at[q], dst_ref=self.y.at[q],
                send_sem=g_s.at[self.w, k - 1], recv_sem=g_r.at[self.w, k - 1],
                device_id=device(sx, to), device_id_type=MESH)

        def start(self):
            for k in range(1, nq):
                self.plane(k).start()

        def second(self):
            for k in range(1, nq):
                self.plane(k).wait()
            part = self.x[q]
            for k in range(1, nq):
                part = part + self.a[k - 1]
            self.z[...] = part
            for k in range(1, nsx):
                self.line(k).start()
            self.b[sx] = part

        def third(self):
            for k in range(1, nsx):
                self.line(k).wait()
            part = self.b[0]
            for k in range(1, nsx):
                part = part + self.b[k]
            self.y[q] = part * (1.0 / total_sites)
            for k in range(1, nq):
                self.back(k).start()

        def finish(self):
            for k in range(1, nq):
                self.back(k).wait()

    reduce_ss = (ReduceFlat if flat else Reduce)(0, ss_x, ss_a, ss_b, ss_z, ss_y)
    reduce_1 = (ReduceFlat if flat else Reduce)(1, r1_x, r1_a, r1_b, r1_z, r1_y)
    reduce_2 = (ReduceFlat if flat else Reduce)(2, r2_x, r2_a, r2_b, r2_z, r2_y)

    halo_start(ppad, pos_s, pos_r)
    for load in loads[1::2]:
        load.wait()
    halo_start(vpad, v1_s, v1_r)

    def split(a, b):
        high, low = halves(vpad[a, b])
        vbf[a, b, 0:width] = high
        vbf[a, b, width : 2 * width] = low
        return high, low

    def interior(a, b):
        return (a >= 1) & (a <= tx) & (b >= 1) & (b <= ty)

    def split_halo():
        for b in range(ty + 2):
            split(0, b)
            split(tx + 1, b)
        for a in range(1, tx + 1):
            split(a, 0)
            split(a, ty + 1)

    first_rows = pl.ds(prev, width)
    cur_rows = pl.ds(prev + width, width)
    second_rows = pl.ds(prev + 2 * width, width)

    @pl.loop(0, tiles)
    def _(t):
        high, low = split(t // ty + 1, lax.rem(t, ty) + 1)
        shi[t, cur_rows] = high
        slo[t, cur_rows] = low
        shi[t, first_rows] = jnp.zeros((width, 256), BF16)
        slo[t, first_rows] = jnp.zeros((width, 256), BF16)

    rowbuf[...] = jnp.zeros_like(rowbuf)
    halo_wait(ppad, pos_s, pos_r)

    def place_terms(slot, terms):
        for k, term in enumerate(terms):
            if term is not None:
                rowbuf[slot, k : k + 1, :] = term

    def near_factors(a, b):
        x, y = ppad[a, b, 0:1, :], ppad[a, b, 1:2, :]
        xs, ys, norm = thirds(x), thirds(y), thirds(x * x + y * y)
        one = jnp.ones((1, 256), F32)
        terms = [*norm, one, one, one]
        for p in (xs, ys):
            terms += [p[0], p[0], p[1], p[1], p[0], p[2]]
        place_terms(b, terms)
        near_m[a, b] = jnp.transpose(rowbuf[b]).astype(BF16)

    def own_factors(oa, ob):
        for code in range(9):
            da, db = code // 3 - 1, code % 3 - 1
            x = ppad[oa, ob, 0:1, :] - float(da)
            y = ppad[oa, ob, 1:2, :] - float(db)
            xs, ys, norm = thirds(x), thirds(y), thirds(x * x + y * y)
            one = jnp.ones((1, 256), F32)
            terms = [one, one, one, *norm]
            for p in (xs, ys):
                terms += [-2.0 * p[n] for n in (0, 1, 0, 1, 2, 0)]
            place_terms(code, terms)
            own_m[code] = rowbuf[code].astype(BF16)

    @pl.loop(0, tx + 2)
    def _(a):
        for b in range(ty + 2):
            near_factors(a, b)

    for load in prior_loads:
        load.wait()
    grams[...] = jnp.zeros_like(grams)
    skew[...] = jnp.zeros_like(skew)

    @pl.loop(0, tiles)
    def _(t):
        for h in range(prev // width):
            high, low = halves(stage[h, t])
            shi[t, h * width : (h + 1) * width] = high
            slo[t, h * width : (h + 1) * width] = low

    group_size = 4

    @pl.loop(0, tiles // group_size)
    def _(i):
        high = [shi[i * group_size + n, 0:full] for n in range(group_size)]
        low = [slo[i * group_size + n, 0:full] for n in range(group_size)]
        grams[...] = grams[...] + sum(dot_fast_nt(h, h) for h in high)
        skew[...] = skew[...] + sum(dot_fast_nt(h, l) for h, l in zip(high, low))
    grams[...] = grams[...] + skew[...] + jnp.transpose(skew[...])
    chunk = ss_x.shape[1]
    for r in range(0, prev + width, 4):
        c, i = r // chunk, r % chunk
        row = r if r < prev else r + width
        ss_x[c, i : i + 4] = grams[row : row + 4, :]
    reduce_ss.start()

    def inner(t):
        a, b = t // ty, lax.rem(t, ty)
        return (a >= 1) & (a < tx - 1) & (b >= 1) & (b < ty - 1)

    def make_weights(t, code):
        oa, ob = t // ty + 1, lax.rem(t, ty) + 1
        na, nb = oa + code // 3 - 1, ob + code % 3 - 1
        link = links[code, t // ty, lax.rem(t, ty)].astype(F32) * GAIN
        c4 = link * 4.0
        place = t * 9 + code
        step = 64
        for j in range(0, 256, step):
            sq = dot_fast(near_m[na, nb, j : j + step, :], own_m[code])
            sq = jnp.maximum(sq, 1e-12)
            dist = sq * lax.rsqrt(sq)
            fall = jnp.maximum(1.0 - dist, 0.0)
            two = fall * fall
            high, low = halves((two * two) * (dist * c4 + link))
            khi[place, j : j + step, :] = high
            klo[place, j : j + step, :] = low

    def apply_tile(t, rows):
        oa, ob = t // ty + 1, lax.rem(t, ty) + 1
        both, part = None, None
        for code in range(9):
            na, nb = oa + code // 3 - 1, ob + code % 3 - 1
            one = dot_fast(vbf[na, nb], khi[t * 9 + code])
            two = dot_fast(vbf[na, nb, 0:width], klo[t * 9 + code])
            both = one if both is None else both + one
            part = two if part is None else part + two
        high, low = halves(both[0:width] + both[width : 2 * width] + part)
        shi[t, rows] = high
        slo[t, rows] = low

    @pl.loop(0, tiles)
    def _(t):
        own_factors(t // ty + 1, lax.rem(t, ty) + 1)
        for code in range(9):
            make_weights(t, code)

        @pl.when(t == 3)
        def _():
            reduce_ss.second()

        @pl.when(t == 7)
        def _():
            reduce_ss.third()

        @pl.when(t == 11)
        def _():
            reduce_ss.finish()

    @pl.loop(0, tiles)
    def _(t):
        @pl.when(inner(t))
        def _():
            apply_tile(t, first_rows)
    halo_wait(vpad, v1_s, v1_r)
    split_halo()

    @pl.loop(0, tiles)
    def _(t):
        @pl.when(jnp.logical_not(inner(t)))
        def _():
            apply_tile(t, first_rows)

    def products(rows, extra):
        image[...] = jnp.zeros_like(image)

        @pl.loop(0, tiles // group_size)
        def _(i):
            total, mine = None, None
            for n in range(group_size):
                t = i * group_size + n
                high, low = shi[t, rows], slo[t, rows]
                both = jnp.concatenate([high, low], axis=0)
                one = dot_fast_nt(both, shi[t, 0:full])
                one = one[0:width] + one[width : 2 * width] + dot_fast_nt(high, slo[t, 0:full])
                total = one if total is None else total + one
                if extra:
                    one = dot_fast_nt(both, high)
                    one = one[0:width] + one[width : 2 * width] + dot_fast_nt(high, low)
                    mine = one if mine is None else mine + one
            image[:, 0:full] = image[:, 0:full] + total
            if extra:
                image[:, full : full + width] = image[:, full : full + width] + mine

    def reduce_now(reduce, columns):
        chunk = reduce.x.shape[1]
        chunks = reduce.x.shape[0]
        for c in range(chunks):
            reduce.x[c] = image[c * chunk : (c + 1) * chunk, 0:columns]
        reduce.start()
        reduce.second()
        reduce.third()
        reduce.finish()
        for c in range(chunks):
            image[c * chunk : (c + 1) * chunk, 0:columns] = reduce.y[c]
        return image[:, 0:columns]

    products(first_rows, False)
    chunk = ss_x.shape[1]
    grams[prev : prev + width, :] = jnp.zeros((width, full), F32)
    for r in range(0, prev + width, 4):
        c, i = r // chunk, r % chunk
        row = r if r < prev else r + width
        grams[row : row + 4, :] = ss_y[c, i : i + 4]
    lane = lax.broadcasted_iota(jnp.int32, (width, full), 1)
    inside = (lane >= prev) & (lane < prev + width)
    tlane = lax.broadcasted_iota(jnp.int32, (full, full), 1)
    grams[...] = jnp.where((tlane >= prev) & (tlane < prev + width), 0.0, grams[...])

    red = reduce_now(reduce_1, full)
    coef = jnp.where(inside, 0.0, red)
    over = dot_nn(coef, grams[...])
    gram = red[:, prev : prev + width] + dot_nt(over - 2.0 * coef, coef)
    lower = inverse_factor(gram)
    image[:, 0:full] = -dot_nn(lower, coef)
    image[:, prev : prev + width] = lower
    cross = dot_nn(lower, coef - over)
    mix_high, mix_low = halves(image[:, 0:full])
    mix = jnp.concatenate([mix_high, mix_low], axis=0)

    def mixed(mix, mix_high, high, low):
        both = dot_fast(mix, high)
        return both[0:width] + both[width : 2 * width] + dot_fast(mix_high, low)

    def first_copy(t):
        a, b = t // ty, lax.rem(t, ty)
        return pltpu.make_async_copy(
            vpad.at[a + 1, b + 1], first_out.at[:, a, b], out_sem.at[0, t])

    def second_copy(t):
        a, b = t // ty, lax.rem(t, ty)
        return pltpu.make_async_copy(
            stage.at[0, t], second_out.at[:, a, b], out_sem.at[1, t])

    @pl.loop(0, tiles // group_size)
    def _(i):
        for n in range(group_size):
            t = i * group_size + n
            a, b = t // ty + 1, lax.rem(t, ty) + 1
            fresh = mixed(mix, mix_high, shi[t, 0:full], slo[t, 0:full])
            vpad[a, b] = fresh
            high, low = halves(fresh)
            shi[t, first_rows] = high
            slo[t, first_rows] = low
            vbf[a, b, 0:width] = high
            vbf[a, b, width : 2 * width] = low

    halo_start(vpad, v2_s, v2_r)

    @pl.loop(0, tiles)
    def _(t):
        first_copy(t).start()
    rowi = lax.broadcasted_iota(jnp.int32, (width, full), 0)
    cross = jnp.where(lane == rowi + prev, 1.0, cross)
    grams[prev : prev + width, :] = cross
    grams[:, prev : prev + width] = jnp.transpose(cross)

    @pl.loop(0, tiles)
    def _(t):
        @pl.when(inner(t))
        def _():
            apply_tile(t, second_rows)
    halo_wait(vpad, v2_s, v2_r)
    split_halo()

    @pl.loop(0, tiles)
    def _(t):
        @pl.when(jnp.logical_not(inner(t)))
        def _():
            apply_tile(t, second_rows)

    products(second_rows, True)
    red = reduce_now(reduce_2, full + 128)
    coef = red[:, 0:full]
    over = dot_nn(coef, grams[...])
    gram = red[:, full : full + width] + dot_nt(over - 2.0 * coef, coef)
    lower = inverse_factor(gram)
    main_high, main_low = halves(-dot_nn(lower, coef))
    tail_high, tail_low = halves(lower)
    main = jnp.concatenate([main_high, main_low], axis=0)
    tail = jnp.concatenate([tail_high, tail_low], axis=0)

    @pl.loop(0, tiles // group_size)
    def _(i):
        for n in range(group_size):
            t = i * group_size + n
            stage[0, t] = mixed(main, main_high, shi[t, 0:full], slo[t, 0:full]) + mixed(
                tail, tail_high, shi[t, second_rows], slo[t, second_rows])
            second_copy(t).start()

    @pl.loop(0, tiles)
    def _(t):
        first_copy(t).wait()
        second_copy(t).wait()


def on_device(nsx, nsy, nsz, prior, current, site_xy, links):
    prev, tx, ty, ts = prior.shape
    width = current.shape[0]
    tiles = tx * ty
    nq = nsy * nsz
    full = prev + 2 * width

    def reduce_bufs(rows, cols):
        if is_flat(nsx, nq):
            count = nsx * nq
            chunk = rows // count
            return [
                pltpu.VMEM((count, chunk, cols), F32),
                pltpu.VMEM((count - 1, chunk, cols), F32),
                pltpu.VMEM((8, 128), F32),
                pltpu.VMEM((8, 128), F32),
                pltpu.VMEM((count, chunk, cols), F32),
            ]
        chunk = rows // nq
        return [
            pltpu.VMEM((nq, chunk, cols), F32),
            pltpu.VMEM((nq - 1, chunk, cols), F32),
            pltpu.VMEM((nsx, chunk, cols), F32),
            pltpu.VMEM((chunk, cols), F32),
            pltpu.VMEM((nq, chunk, cols), F32),
        ]

    dma = pltpu.SemaphoreType.DMA
    peers = (nsx * nq if is_flat(nsx, nq) else nq) - 1
    first, second = pl.pallas_call(
        functools.partial(body, nsx, nsy, nsz, tx, ty),
        out_shape=[jax.ShapeDtypeStruct(current.shape, F32)] * 2,
        in_specs=[
            pl.BlockSpec(memory_space=pltpu.SMEM),
            pl.BlockSpec(memory_space=pl.ANY),
            pl.BlockSpec(memory_space=pl.ANY),
            pl.BlockSpec(memory_space=pl.ANY),
        ],
        out_specs=[pl.BlockSpec(memory_space=pl.ANY)] * 2,
        scratch_shapes=[
            pltpu.VMEM((tiles * 9, ts, ts), BF16),
            pltpu.VMEM((tiles * 9, ts, ts), BF16),
            pltpu.VMEM((tiles, full + width, ts), BF16),
            pltpu.VMEM((tiles, full + width, ts), BF16),
            pltpu.VMEM((tx + 2, ty + 2, width, ts), F32),
            pltpu.VMEM((tx + 2, ty + 2, 2 * width, ts), BF16),
            pltpu.VMEM((tx + 2, ty + 2, 2, ts), F32),
            pltpu.VMEM((9, 32, ts), F32),
            pltpu.VMEM((tx + 2, ty + 2, ts, 32), BF16),
            pltpu.VMEM((9, 32, ts), BF16),
            pltpu.VMEM((prev // width, tiles, width, ts), F32),
            pltpu.VMEM((width, full + 128), F32),
            pltpu.VMEM((full, full), F32),
            pltpu.VMEM((full, full), F32),
        ]
        + reduce_bufs(prev + width, full)
        + reduce_bufs(width, full)
        + reduce_bufs(width, full + 128)
        + [dma((tiles,))] * 2
        + [dma((prev // width, tiles)), dma((2, tiles))]
        + [dma((8,))] * 6
        + [dma((3, peers))] * 2
        + [dma((3, nsx - 1))] * 2
        + [dma((3, peers))] * 2,
        compiler_params=pltpu.CompilerParams(
            collective_id=0, has_side_effects=True, vmem_limit_bytes=62 * 1024 * 1024),
    )(links, prior, current, site_xy)
    return first, second


def solution(mesh):
    sizes = mesh.shape
    whole = P(None, ("groups", "sx"), ("sy", "sz"), None)
    return jax.shard_map(
        functools.partial(on_device, sizes["sx"], sizes["sy"], sizes["sz"]),
        mesh=mesh,
        in_specs=(whole, whole, whole, P(None, ("groups", "sx"), ("sy", "sz"))),
        out_specs=(whole, whole),
        check_vma=False,
    )
```

```python
import functools

import jax
import jax.numpy as jnp
from jax import lax
from jax.experimental import pallas as pl
from jax.experimental.pallas import tpu as pltpu
from jax.sharding import PartitionSpec as P

GAIN = 0.0625
MESH = pl.DeviceIdType.MESH
F32 = jnp.float32
BF16 = jnp.bfloat16
HIGH = lax.Precision.HIGHEST
DIRS = [(da, db) for da in (-1, 0, 1) for db in (-1, 0, 1) if (da, db) != (0, 0)]


def dot_nn(left, right):
    return lax.dot_general(
        left, right, (((1,), (0,)), ((), ())), precision=HIGH, preferred_element_type=F32
    )


def dot_nt(left, right):
    return lax.dot_general(
        left, right, (((1,), (1,)), ((), ())), precision=HIGH, preferred_element_type=F32
    )


def dot_fast(left, right):
    return lax.dot_general(
        left, right, (((1,), (0,)), ((), ())), preferred_element_type=F32
    )


def dot_fast_nt(left, right):
    return lax.dot_general(
        left, right, (((1,), (1,)), ((), ())), preferred_element_type=F32
    )


def halves(value):
    high = value.astype(BF16)
    return high, (value - high.astype(F32)).astype(BF16)


def thirds(value):
    one = value.astype(BF16).astype(F32)
    rest = value - one
    two = rest.astype(BF16).astype(F32)
    return one, two, rest - two


def inverse_factor(gram):
    size = gram.shape[0]
    rows = lax.broadcasted_iota(jnp.int32, (size, size), 0)
    cols = lax.broadcasted_iota(jnp.int32, (size, size), 1)
    eye = jnp.where(rows == cols, 1.0, 0.0).astype(F32)
    work = jnp.concatenate([eye, gram], axis=1)
    wide = 2 * size
    rowid = lax.broadcasted_iota(jnp.int32, (size, wide), 0)
    pivots = jnp.ones((size, wide), F32)
    panel = 8
    for base in range(0, size, panel):
        cast = [
            jnp.broadcast_to(work[:, size + base + c : size + base + c + 1], (size, wide))
            for c in range(panel)
        ]
        for c in range(panel):
            k = base + c
            pivot = cast[c][k : k + 1, :]
            pivots = jnp.where(rowid == k, pivot, pivots)
            factor = jnp.where(rowid > k, cast[c] * (1.0 / pivot), 0.0)
            work = work - factor * work[k : k + 1, :]
            for d in range(c + 1, panel):
                cast[d] = cast[d] - factor * cast[d][k : k + 1, :]
    scaled = work * lax.rsqrt(pivots)
    return scaled[:, :size]


def is_flat(nsx, nq):
    return nsx * nq <= 4


def body(
    nsx, nsy, nsz, tx, ty,
    links, prior_in, cur_in, pos_in,
    first_out, second_out,
    khi, klo, shi, slo, vpad, vbf, ppad, rowbuf, near_m, own_m, stage, image, grams, skew,
    ss_x, ss_a, ss_b, ss_z, ss_y,
    r1_x, r1_a, r1_b, r1_z, r1_y,
    r2_x, r2_a, r2_b, r2_z, r2_y,
    cur_sem, pos_sem, prior_sem, out_sem, pos_s, pos_r, v1_s, v1_r, v2_s, v2_r, pl_s, pl_r, z_s, z_r, g_s, g_r,
):
    nq = nsy * nsz
    count = nsx * nq
    flat = is_flat(nsx, nq)
    group = lax.axis_index("groups")
    sx = lax.axis_index("sx")
    q = lax.axis_index("sy") * nsz + lax.axis_index("sz")
    prev = prior_in.shape[0]
    width = cur_in.shape[0]
    full = prev + 2 * width
    total_sites = float(tx * ty * 256 * nsx * nq)
    tiles = tx * ty

    def device(s, p):
        return (group, s, p // nsz, lax.rem(p, nsz))

    def exists(d):
        s, p = sx + d[0], q + d[1]
        return (s >= 0) & (s < nsx) & (p >= 0) & (p < nq)

    loads, prior_loads = [], []
    for t in range(tiles):
        a, b = t // ty, t % ty
        loads.append(pltpu.make_async_copy(
            pos_in.at[:, a, b], ppad.at[a + 1, b + 1], pos_sem.at[t]))
        loads.append(pltpu.make_async_copy(
            cur_in.at[:, a, b], vpad.at[a + 1, b + 1], cur_sem.at[t]))
        for h in range(prev // width):
            prior_loads.append(pltpu.make_async_copy(
                prior_in.at[pl.ds(h * width, width), a, b], stage.at[h, t],
                prior_sem.at[h, t]))
    for a in range(tx + 2):
        for b in range(ty + 2):
            if a in (0, tx + 1) or b in (0, ty + 1):
                vpad[a, b] = jnp.zeros((width, 256), F32)
                ppad[a, b] = jnp.zeros((2, 256), F32)
    for load in loads:
        load.start()
    for load in prior_loads:
        load.start()

    barrier = pltpu.get_barrier_semaphore()
    expected = jnp.int32(count - 1 if flat else nq - 1 + nsx - 1)
    for d in DIRS:
        ok = exists(d)
        expected = expected + jnp.where(ok, 1, 0)

        @pl.when(ok)
        def _(d=d):
            pl.semaphore_signal(
                barrier, inc=1, device_id=device(sx + d[0], q + d[1]), device_id_type=MESH)
    if flat:
        for k in range(1, count):
            to = lax.rem(sx * nq + q + k, count)
            pl.semaphore_signal(
                barrier, inc=1, device_id=device(to // nq, lax.rem(to, nq)), device_id_type=MESH)
    else:
        for k in range(1, nq):
            pl.semaphore_signal(
                barrier, inc=1, device_id=device(sx, lax.rem(q + k, nq)), device_id_type=MESH)
        for k in range(1, nsx):
            pl.semaphore_signal(
                barrier, inc=1, device_id=device(lax.rem(sx + k, nsx), q), device_id_type=MESH)
    pl.semaphore_wait(barrier, expected)
    for load in loads[0::2]:
        load.wait()

    def pick(shift, count):
        src = {-1: pl.ds(1, 1), 0: pl.ds(1, count), 1: pl.ds(count, 1)}[shift]
        dst = {-1: pl.ds(count + 1, 1), 0: pl.ds(1, count), 1: pl.ds(0, 1)}[shift]
        return src, dst

    def halo_copy(ref, i, send, recv):
        d = DIRS[i]
        (sa, da), (sb, db) = pick(d[0], tx), pick(d[1], ty)
        return pltpu.make_async_remote_copy(
            src_ref=ref.at[sa, sb], dst_ref=ref.at[da, db],
            send_sem=send.at[i], recv_sem=recv.at[i],
            device_id=device(sx + d[0], q + d[1]), device_id_type=MESH)

    def halo_start(ref, send, recv):
        for i, d in enumerate(DIRS):
            @pl.when(exists(d))
            def _(i=i):
                halo_copy(ref, i, send, recv).start()

    def halo_wait(ref, send, recv):
        for i, d in enumerate(DIRS):
            @pl.when(exists(d))
            def _(i=i):
                halo_copy(ref, i, send, recv).wait_send()

            @pl.when(exists((-d[0], -d[1])))
            def _(i=i):
                halo_copy(ref, i, send, recv).wait_recv()

    me = sx * nq + q

    def member(p):
        return device(p // nq, lax.rem(p, nq))

    class ReduceFlat:
        def __init__(self, which, x, a, b, z, y):
            self.w, self.x, self.a, self.y = which, x, a, y

        def scatter(self, k):
            to = lax.rem(me + k, count)
            return pltpu.make_async_remote_copy(
                src_ref=self.x.at[to], dst_ref=self.a.at[k - 1],
                send_sem=pl_s.at[self.w, k - 1], recv_sem=pl_r.at[self.w, k - 1],
                device_id=member(to), device_id_type=MESH)

        def back(self, k):
            to = lax.rem(me + k, count)
            return pltpu.make_async_remote_copy(
                src_ref=self.y.at[me], dst_ref=self.y.at[me],
                send_sem=g_s.at[self.w, k - 1], recv_sem=g_r.at[self.w, k - 1],
                device_id=member(to), device_id_type=MESH)

        def start(self):
            for k in range(1, count):
                self.scatter(k).start()

        def second(self):
            part = self.x[me]
            for k in range(1, count):
                self.scatter(k).wait_recv()
            for k in range(1, count):
                part = part + self.a[k - 1]
            self.y[me] = part * (1.0 / total_sites)
            for k in range(1, count):
                self.back(k).start()

        def third(self):
            for k in range(1, count):
                self.scatter(k).wait_send()

        def finish(self):
            for k in range(1, count):
                self.back(k).wait()

    class Reduce:
        def __init__(self, which, x, a, b, z, y):
            self.w, self.x, self.a, self.b, self.z, self.y = which, x, a, b, z, y

        def plane(self, k):
            to = lax.rem(q + k, nq)
            return pltpu.make_async_remote_copy(
                src_ref=self.x.at[to], dst_ref=self.a.at[k - 1],
                send_sem=pl_s.at[self.w, k - 1], recv_sem=pl_r.at[self.w, k - 1],
                device_id=device(sx, to), device_id_type=MESH)

        def line(self, k):
            to = lax.rem(sx + k, nsx)
            return pltpu.make_async_remote_copy(
                src_ref=self.z, dst_ref=self.b.at[sx],
                send_sem=z_s.at[self.w, k - 1], recv_sem=z_r.at[self.w, k - 1],
                device_id=device(to, q), device_id_type=MESH)

        def back(self, k):
            to = lax.rem(q + k, nq)
            return pltpu.make_async_remote_copy(
                src_ref=self.y.at[q], dst_ref=self.y.at[q],
                send_sem=g_s.at[self.w, k - 1], recv_sem=g_r.at[self.w, k - 1],
                device_id=device(sx, to), device_id_type=MESH)

        def start(self):
            for k in range(1, nq):
                self.plane(k).start()

        def second(self):
            for k in range(1, nq):
                self.plane(k).wait()
            part = self.x[q]
            for k in range(1, nq):
                part = part + self.a[k - 1]
            self.z[...] = part
            for k in range(1, nsx):
                self.line(k).start()
            self.b[sx] = part

        def third(self):
            for k in range(1, nsx):
                self.line(k).wait()
            part = self.b[0]
            for k in range(1, nsx):
                part = part + self.b[k]
            self.y[q] = part * (1.0 / total_sites)
            for k in range(1, nq):
                self.back(k).start()

        def finish(self):
            for k in range(1, nq):
                self.back(k).wait()

    reduce_ss = (ReduceFlat if flat else Reduce)(0, ss_x, ss_a, ss_b, ss_z, ss_y)
    reduce_1 = (ReduceFlat if flat else Reduce)(1, r1_x, r1_a, r1_b, r1_z, r1_y)
    reduce_2 = (ReduceFlat if flat else Reduce)(2, r2_x, r2_a, r2_b, r2_z, r2_y)

    halo_start(ppad, pos_s, pos_r)
    for load in loads[1::2]:
        load.wait()
    halo_start(vpad, v1_s, v1_r)

    def split(a, b):
        high, low = halves(vpad[a, b])
        vbf[a, b, 0:width] = high
        vbf[a, b, width : 2 * width] = low
        return high, low

    def interior(a, b):
        return (a >= 1) & (a <= tx) & (b >= 1) & (b <= ty)

    def split_halo():
        for b in range(ty + 2):
            split(0, b)
            split(tx + 1, b)
        for a in range(1, tx + 1):
            split(a, 0)
            split(a, ty + 1)

    first_rows = pl.ds(prev, width)
    cur_rows = pl.ds(prev + width, width)
    second_rows = pl.ds(prev + 2 * width, width)

    @pl.loop(0, tiles)
    def _(t):
        high, low = split(t // ty + 1, lax.rem(t, ty) + 1)
        shi[t, cur_rows] = high
        slo[t, cur_rows] = low
        shi[t, first_rows] = jnp.zeros((width, 256), BF16)
        slo[t, first_rows] = jnp.zeros((width, 256), BF16)

    rowbuf[...] = jnp.zeros_like(rowbuf)
    halo_wait(ppad, pos_s, pos_r)

    def place_terms(slot, terms):
        for k, term in enumerate(terms):
            if term is not None:
                rowbuf[slot, k : k + 1, :] = term

    def near_factors(a, b):
        x, y = ppad[a, b, 0:1, :], ppad[a, b, 1:2, :]
        xs, ys, norm = thirds(x), thirds(y), thirds(x * x + y * y)
        one = jnp.ones((1, 256), F32)
        terms = [*norm, one, one, one]
        for p in (xs, ys):
            terms += [p[0], p[0], p[1], p[1], p[0], p[2]]
        place_terms(b, terms)
        near_m[a, b] = jnp.transpose(rowbuf[b]).astype(BF16)

    def own_factors(oa, ob):
        for code in range(9):
            da, db = code // 3 - 1, code % 3 - 1
            x = ppad[oa, ob, 0:1, :] - float(da)
            y = ppad[oa, ob, 1:2, :] - float(db)
            xs, ys, norm = thirds(x), thirds(y), thirds(x * x + y * y)
            one = jnp.ones((1, 256), F32)
            terms = [one, one, one, *norm]
            for p in (xs, ys):
                terms += [-2.0 * p[n] for n in (0, 1, 0, 1, 2, 0)]
            place_terms(code, terms)
            own_m[code] = rowbuf[code].astype(BF16)

    @pl.loop(0, tx + 2)
    def _(a):
        for b in range(ty + 2):
            near_factors(a, b)

    for load in prior_loads:
        load.wait()
    grams[...] = jnp.zeros_like(grams)
    skew[...] = jnp.zeros_like(skew)

    @pl.loop(0, tiles)
    def _(t):
        for h in range(prev // width):
            high, low = halves(stage[h, t])
            shi[t, h * width : (h + 1) * width] = high
            slo[t, h * width : (h + 1) * width] = low

    group_size = 4

    @pl.loop(0, tiles // group_size)
    def _(i):
        high = [shi[i * group_size + n, 0:full] for n in range(group_size)]
        low = [slo[i * group_size + n, 0:full] for n in range(group_size)]
        grams[...] = grams[...] + sum(dot_fast_nt(h, h) for h in high)
        skew[...] = skew[...] + sum(dot_fast_nt(h, l) for h, l in zip(high, low))
    grams[...] = grams[...] + skew[...] + jnp.transpose(skew[...])
    chunk = ss_x.shape[1]
    for r in range(0, prev + width, 4):
        c, i = r // chunk, r % chunk
        row = r if r < prev else r + width
        ss_x[c, i : i + 4] = grams[row : row + 4, :]
    reduce_ss.start()

    halo_wait(vpad, v1_s, v1_r)
    split_halo()

    def make_weights(t, code):
        oa, ob = t // ty + 1, lax.rem(t, ty) + 1
        na, nb = oa + code // 3 - 1, ob + code % 3 - 1
        link = links[code, t // ty, lax.rem(t, ty)].astype(F32) * GAIN
        c4 = link * 4.0
        place = t * 9 + code
        step = 64
        for j in range(0, 256, step):
            sq = dot_fast(near_m[na, nb, j : j + step, :], own_m[code])
            sq = jnp.maximum(sq, 1e-12)
            dist = sq * lax.rsqrt(sq)
            fall = jnp.maximum(1.0 - dist, 0.0)
            two = fall * fall
            high, low = halves((two * two) * (dist * c4 + link))
            khi[place, j : j + step, :] = high
            klo[place, j : j + step, :] = low

    def apply_tile(t, rows):
        oa, ob = t // ty + 1, lax.rem(t, ty) + 1
        both, part = None, None
        for code in range(9):
            na, nb = oa + code // 3 - 1, ob + code % 3 - 1
            one = dot_fast(vbf[na, nb], khi[t * 9 + code])
            two = dot_fast(vbf[na, nb, 0:width], klo[t * 9 + code])
            both = one if both is None else both + one
            part = two if part is None else part + two
        high, low = halves(both[0:width] + both[width : 2 * width] + part)
        shi[t, rows] = high
        slo[t, rows] = low

    @pl.loop(0, tiles)
    def _(t):
        own_factors(t // ty + 1, lax.rem(t, ty) + 1)
        for code in range(9):
            make_weights(t, code)
        apply_tile(t, first_rows)

        @pl.when(t == 3)
        def _():
            reduce_ss.second()

        @pl.when(t == 7)
        def _():
            reduce_ss.third()

        @pl.when(t == 11)
        def _():
            reduce_ss.finish()

    def products(rows, extra):
        image[...] = jnp.zeros_like(image)

        @pl.loop(0, tiles // group_size)
        def _(i):
            total, mine = None, None
            for n in range(group_size):
                t = i * group_size + n
                high, low = shi[t, rows], slo[t, rows]
                both = jnp.concatenate([high, low], axis=0)
                one = dot_fast_nt(both, shi[t, 0:full])
                one = one[0:width] + one[width : 2 * width] + dot_fast_nt(high, slo[t, 0:full])
                total = one if total is None else total + one
                if extra:
                    one = dot_fast_nt(both, high)
                    one = one[0:width] + one[width : 2 * width] + dot_fast_nt(high, low)
                    mine = one if mine is None else mine + one
            image[:, 0:full] = image[:, 0:full] + total
            if extra:
                image[:, full : full + width] = image[:, full : full + width] + mine

    def reduce_now(reduce, columns):
        chunk = reduce.x.shape[1]
        chunks = reduce.x.shape[0]
        for c in range(chunks):
            reduce.x[c] = image[c * chunk : (c + 1) * chunk, 0:columns]
        reduce.start()
        reduce.second()
        reduce.third()
        reduce.finish()
        for c in range(chunks):
            image[c * chunk : (c + 1) * chunk, 0:columns] = reduce.y[c]
        return image[:, 0:columns]

    products(first_rows, False)
    chunk = ss_x.shape[1]
    grams[prev : prev + width, :] = jnp.zeros((width, full), F32)
    for r in range(0, prev + width, 4):
        c, i = r // chunk, r % chunk
        row = r if r < prev else r + width
        grams[row : row + 4, :] = ss_y[c, i : i + 4]
    lane = lax.broadcasted_iota(jnp.int32, (width, full), 1)
    inside = (lane >= prev) & (lane < prev + width)
    tlane = lax.broadcasted_iota(jnp.int32, (full, full), 1)
    grams[...] = jnp.where((tlane >= prev) & (tlane < prev + width), 0.0, grams[...])

    red = reduce_now(reduce_1, full)
    coef = jnp.where(inside, 0.0, red)
    over = dot_nn(coef, grams[...])
    gram = red[:, prev : prev + width] + dot_nt(over - 2.0 * coef, coef)
    lower = inverse_factor(gram)
    image[:, 0:full] = -dot_nn(lower, coef)
    image[:, prev : prev + width] = lower
    cross = dot_nn(lower, coef - over)
    mix_high, mix_low = halves(image[:, 0:full])
    mix = jnp.concatenate([mix_high, mix_low], axis=0)

    def mixed(mix, mix_high, high, low):
        both = dot_fast(mix, high)
        return both[0:width] + both[width : 2 * width] + dot_fast(mix_high, low)

    def first_copy(t):
        a, b = t // ty, lax.rem(t, ty)
        return pltpu.make_async_copy(
            vpad.at[a + 1, b + 1], first_out.at[:, a, b], out_sem.at[0, t])

    def second_copy(t):
        a, b = t // ty, lax.rem(t, ty)
        return pltpu.make_async_copy(
            stage.at[0, t], second_out.at[:, a, b], out_sem.at[1, t])

    @pl.loop(0, tiles // group_size)
    def _(i):
        for n in range(group_size):
            t = i * group_size + n
            a, b = t // ty + 1, lax.rem(t, ty) + 1
            fresh = mixed(mix, mix_high, shi[t, 0:full], slo[t, 0:full])
            vpad[a, b] = fresh
            high, low = halves(fresh)
            shi[t, first_rows] = high
            slo[t, first_rows] = low
            vbf[a, b, 0:width] = high
            vbf[a, b, width : 2 * width] = low

    halo_start(vpad, v2_s, v2_r)

    @pl.loop(0, tiles)
    def _(t):
        first_copy(t).start()
    rowi = lax.broadcasted_iota(jnp.int32, (width, full), 0)
    cross = jnp.where(lane == rowi + prev, 1.0, cross)
    grams[prev : prev + width, :] = cross
    grams[:, prev : prev + width] = jnp.transpose(cross)

    def inner(t):
        a, b = t // ty, lax.rem(t, ty)
        return (a >= 1) & (a < tx - 1) & (b >= 1) & (b < ty - 1)

    @pl.loop(0, tiles)
    def _(t):
        @pl.when(inner(t))
        def _():
            apply_tile(t, second_rows)
    halo_wait(vpad, v2_s, v2_r)
    split_halo()

    @pl.loop(0, tiles)
    def _(t):
        @pl.when(jnp.logical_not(inner(t)))
        def _():
            apply_tile(t, second_rows)

    products(second_rows, True)
    red = reduce_now(reduce_2, full + 128)
    coef = red[:, 0:full]
    over = dot_nn(coef, grams[...])
    gram = red[:, full : full + width] + dot_nt(over - 2.0 * coef, coef)
    lower = inverse_factor(gram)
    main_high, main_low = halves(-dot_nn(lower, coef))
    tail_high, tail_low = halves(lower)
    main = jnp.concatenate([main_high, main_low], axis=0)
    tail = jnp.concatenate([tail_high, tail_low], axis=0)

    @pl.loop(0, tiles // group_size)
    def _(i):
        for n in range(group_size):
            t = i * group_size + n
            stage[0, t] = mixed(main, main_high, shi[t, 0:full], slo[t, 0:full]) + mixed(
                tail, tail_high, shi[t, second_rows], slo[t, second_rows])
            second_copy(t).start()

    @pl.loop(0, tiles)
    def _(t):
        first_copy(t).wait()
        second_copy(t).wait()


def on_device(nsx, nsy, nsz, prior, current, site_xy, links):
    prev, tx, ty, ts = prior.shape
    width = current.shape[0]
    tiles = tx * ty
    nq = nsy * nsz
    full = prev + 2 * width

    def reduce_bufs(rows, cols):
        if is_flat(nsx, nq):
            count = nsx * nq
            chunk = rows // count
            return [
                pltpu.VMEM((count, chunk, cols), F32),
                pltpu.VMEM((count - 1, chunk, cols), F32),
                pltpu.VMEM((8, 128), F32),
                pltpu.VMEM((8, 128), F32),
                pltpu.VMEM((count, chunk, cols), F32),
            ]
        chunk = rows // nq
        return [
            pltpu.VMEM((nq, chunk, cols), F32),
            pltpu.VMEM((nq - 1, chunk, cols), F32),
            pltpu.VMEM((nsx, chunk, cols), F32),
            pltpu.VMEM((chunk, cols), F32),
            pltpu.VMEM((nq, chunk, cols), F32),
        ]

    dma = pltpu.SemaphoreType.DMA
    peers = (nsx * nq if is_flat(nsx, nq) else nq) - 1
    first, second = pl.pallas_call(
        functools.partial(body, nsx, nsy, nsz, tx, ty),
        out_shape=[jax.ShapeDtypeStruct(current.shape, F32)] * 2,
        in_specs=[
            pl.BlockSpec(memory_space=pltpu.SMEM),
            pl.BlockSpec(memory_space=pl.ANY),
            pl.BlockSpec(memory_space=pl.ANY),
            pl.BlockSpec(memory_space=pl.ANY),
        ],
        out_specs=[pl.BlockSpec(memory_space=pl.ANY)] * 2,
        scratch_shapes=[
            pltpu.VMEM((tiles * 9, ts, ts), BF16),
            pltpu.VMEM((tiles * 9, ts, ts), BF16),
            pltpu.VMEM((tiles, full + width, ts), BF16),
            pltpu.VMEM((tiles, full + width, ts), BF16),
            pltpu.VMEM((tx + 2, ty + 2, width, ts), F32),
            pltpu.VMEM((tx + 2, ty + 2, 2 * width, ts), BF16),
            pltpu.VMEM((tx + 2, ty + 2, 2, ts), F32),
            pltpu.VMEM((9, 32, ts), F32),
            pltpu.VMEM((tx + 2, ty + 2, ts, 32), BF16),
            pltpu.VMEM((9, 32, ts), BF16),
            pltpu.VMEM((prev // width, tiles, width, ts), F32),
            pltpu.VMEM((width, full + 128), F32),
            pltpu.VMEM((full, full), F32),
            pltpu.VMEM((full, full), F32),
        ]
        + reduce_bufs(prev + width, full)
        + reduce_bufs(width, full)
        + reduce_bufs(width, full + 128)
        + [dma((tiles,))] * 2
        + [dma((prev // width, tiles)), dma((2, tiles))]
        + [dma((8,))] * 6
        + [dma((3, peers))] * 2
        + [dma((3, nsx - 1))] * 2
        + [dma((3, peers))] * 2,
        compiler_params=pltpu.CompilerParams(
            collective_id=0, has_side_effects=True, vmem_limit_bytes=62 * 1024 * 1024),
    )(links, prior, current, site_xy)
    return first, second


def solution(mesh):
    sizes = mesh.shape
    whole = P(None, ("groups", "sx"), ("sy", "sz"), None)
    return jax.shard_map(
        functools.partial(on_device, sizes["sx"], sizes["sy"], sizes["sz"]),
        mesh=mesh,
        in_specs=(whole, whole, whole, P(None, ("groups", "sx"), ("sy", "sz"))),
        out_specs=(whole, whole),
        check_vma=False,
    )
```
